128 devices in a mesh: dp: 32 (over y, x_lo, z), row: 4 (over x_hi, core).
Axes of the slice: x: 4 (x_hi: 2, x_lo: 2; x = x_hi * 2 + x_lo), y: 4, z: 4, core: 2. Of those that a mesh axis runs over, the one named last changes fastest.
Arguments:
- text: bfloat16 [65536, 1152], P('dp')
- image: bfloat16 [65536, 1152], P(('dp', 'row'))
- positive: int32 [32, 2048], P('dp'), may hold values from 0 to 2047, as said below
- log_temp: float32 [1], replicated, may hold values from 1.8 to 2.8
- bias: float32 [1], replicated, may hold values from -8 to -5
Outputs:
- grad_text: float32 [65536, 1152], P(('dp', 'row'))
- grad_image: float32 [65536, 1152], P(('dp', 'row'))
- loss: float32 [1], replicated
- grad_log_temp: float32 [1], replicated
- grad_bias: float32 [1], replicated
The draws below stay inside these ranges and needn't reach their ends.
Inputs may be any that keep to these rules, and one draw needn't show every extreme that they name: Each row positive[b] names every image row 0 .. 2047 of block b exactly once.
All inputs are finite; a program needn't handle non-finite values.
Results may differ from the reference program's by a relative error of at most 0.003.
Values may be sent and summed in bfloat16 or wider, within the bound.
A program may use at most 128 MiB of HBM per device.

```python
import math
import jax
import jax.numpy as jnp
from jax import lax

E = 1152
STEPS = 2
TXT = 2048
BATCH = 65536
N_DP = 32


def pairing(key):
    base_key, perm_key, strength_key, row_key, dir_key, amp_key = jax.random.split(key, 6)
    base = jax.random.normal(base_key, (BATCH, E), jnp.float32)
    block_keys = jax.random.split(perm_key, N_DP)
    perms = jax.vmap(lambda k: jax.random.permutation(k, TXT))(block_keys)
    block_strength = jnp.exp(jax.random.uniform(strength_key, (N_DP, 1), jnp.float32, math.log(0.1), math.log(3.0)))
    row_factor = jax.random.uniform(row_key, (BATCH, 1), jnp.float32, 0.8, 1.25)
    strength = jnp.repeat(block_strength, TXT, axis=0) * row_factor
    amplitude = jax.random.uniform(amp_key, (N_DP, 1), jnp.float32, 0.0, 0.35)
    direction = jax.random.normal(dir_key, (N_DP, E), jnp.float32)
    shared = jnp.repeat(amplitude * direction, TXT, axis=0)
    return (base, perms.astype(jnp.int32), strength, shared)


def draw_text(key, part):
    base, perms, strength, shared = pairing(key)
    values = base + shared
    return (values * E ** (-0.5)).astype(jnp.bfloat16)


def draw_image(key, part):
    base, perms, strength, shared = pairing(key)
    key = jax.random.fold_in(key, 2)
    noise_key = jax.random.fold_in(key, 0)
    targets = (jnp.arange(N_DP, dtype=jnp.int32)[:, None] * TXT + perms).reshape(-1)
    aligned = jnp.zeros((BATCH, E), jnp.float32).at[targets].set(base)
    noise = jax.random.normal(noise_key, (BATCH, E), jnp.float32)
    values = strength * aligned + noise + shared
    return (values * E ** (-0.5)).astype(jnp.bfloat16)


def draw_positive(key, part):
    base, perms, strength, shared = pairing(key)
    return perms


def setup_inputs(seed: int = 0) -> dict:
    keys = jax.random.split(jax.random.key(seed), 6)
    text = draw_text(jax.random.fold_in(keys[5], 71), 0)
    image = draw_image(jax.random.fold_in(keys[5], 71), 0)
    positive = draw_positive(jax.random.fold_in(keys[5], 71), 0)
    log_temp = jnp.clip(jax.random.uniform(keys[3], (1,), jnp.float32, 1.8, 2.8), 1.8, 2.8)
    bias = jnp.clip(jax.random.uniform(keys[4], (1,), jnp.float32, -8.0, -5.0), -8.0, -5.0)
    return dict(text=text, image=image, positive=positive, log_temp=log_temp, bias=bias)


def unit_rows(values):
    full = values.astype(jnp.float32)
    inverse = lax.rsqrt(lax.optimization_barrier(jnp.sum(full * full, axis=-1, keepdims=True)) + 1e-06)
    return (full * inverse, inverse)

def unit_backward(grad_unit, unit, inverse):
    along = lax.optimization_barrier(jnp.sum(unit * grad_unit, axis=-1, keepdims=True))
    return (grad_unit - unit * along) * inverse

def reference(text, image, positive, log_temp, bias):
    temp = jnp.exp(log_temp[0])
    shift = bias[0]
    text_unit, text_inv = unit_rows(text)
    image_unit, image_inv = unit_rows(image)
    text_blocks = text_unit.astype(jnp.bfloat16).reshape(N_DP, TXT, E)
    image_blocks = image_unit.astype(jnp.bfloat16).reshape(N_DP, TXT, E)
    columns = jnp.arange(TXT, dtype=jnp.int32)

    def visit(carry, block):
        text_acc, sums = carry
        img = lax.dynamic_index_in_dim(image_blocks, block, 0, keepdims=False)
        pos = lax.dynamic_index_in_dim(positive, block, 0, keepdims=False)
        image_acc = jnp.zeros((TXT, E), jnp.float32)
        for step in range(STEPS):
            source = jnp.mod(block - step + N_DP, N_DP).astype(jnp.int32)
            txt = lax.dynamic_index_in_dim(text_blocks, source, 0, keepdims=False)
            cosine = lax.dot_general(txt, img, (((1,), (1,)), ((), ())), preferred_element_type=jnp.float32)
            logits = temp * cosine + shift
            if step == 0:
                label = (pos[:, None] == columns[None, :]).astype(jnp.float32)
            else:
                label = jnp.zeros_like(logits)
            pair_loss = jax.nn.softplus(jnp.where(label > 0.5, -logits, logits))
            slope = jax.nn.sigmoid(logits) - label
            sums = sums + jnp.stack([jnp.sum(pair_loss), jnp.sum(slope * cosine), jnp.sum(slope)])
            slope_low = slope.astype(jnp.bfloat16)
            text_term = temp * jnp.dot(slope_low, img, preferred_element_type=jnp.float32)
            image_acc = image_acc + temp * lax.dot_general(slope_low, txt, (((0,), (0,)), ((), ())), preferred_element_type=jnp.float32)
            old = lax.dynamic_index_in_dim(text_acc, source, 0, keepdims=False)
            text_acc = lax.dynamic_update_index_in_dim(text_acc, old + text_term, source, 0)
        return ((text_acc, sums), image_acc)
    start = (jnp.zeros((N_DP, TXT, E), jnp.float32), jnp.zeros((3,), jnp.float32))
    (text_acc, sums), image_acc = lax.scan(visit, start, jnp.arange(N_DP, dtype=jnp.int32))
    grad_text = unit_backward(text_acc.reshape(BATCH, E), text_unit, text_inv)
    grad_image = unit_backward(image_acc.reshape(BATCH, E), image_unit, image_inv)
    loss = (sums[0] / BATCH).reshape(1)
    grad_log_temp = (temp * sums[1] / BATCH).reshape(1)
    grad_bias = (sums[2] / BATCH).reshape(1)
    return (grad_text, grad_image, loss, grad_log_temp, grad_bias)
```

```python
import functools

import jax
import jax.numpy as jnp
from jax import lax
from jax.experimental import pallas as pl
from jax.experimental.pallas import tpu as pltpu
from jax.sharding import PartitionSpec as P

MESH = pl.DeviceIdType.MESH
NT = (((1,), (1,)), ((), ()))

IMG, IMG_NEXT, TXT, TXT_PREV = 0, 4, 8, 12

(X_IMG, C_IMG, Z_IMG, Z_TXT_OPP, Z_TXT, Z_IMG_OPP, F_IMG, F_NEXT, F_NEXT_OPP, F_PREV_OPP, F_PREV) = range(11)


def kernel(n_dp, text, image, positive, log_temp, bias, grad_text, grad_image, out_sums,
           held, raw, cosines, slopes, pos_cols, sums, step_in, step_out,
           load_sem, raw_sem, send_sem, recv_sem, step_send, step_recv):
    _, parts, chunk, width = held.shape
    rows = parts * chunk
    n_steps = step_in.shape[0]
    dp, row = lax.axis_index("dp"), lax.axis_index("row")
    side = row + 1 - 2 * (row % 2)
    opposite = (row + 2) % 4
    quarter = (row, side, opposite, (side + 2) % 4)
    up, down = (dp + 1) % n_dp, (dp + n_dp - 1) % n_dp
    last_z, first_z = dp % 4 == 3, dp % 4 == 0

    def flipped(bit):
        return dp + bit - 2 * bit * ((dp // bit) % 2)

    partners = [(dp, side), (dp, opposite)]
    bit = 1
    while bit < n_dp:
        partners.append((flipped(bit), row))
        bit *= 2

    barrier = pltpu.get_barrier_semaphore()
    greeted = [(dp, side), (dp, opposite), (up, row), (up, opposite), (down, row), (down, opposite)] + partners[3:]
    for device in greeted:
        pl.semaphore_signal(barrier, inc=1, device_id=device, device_id_type=MESH)

    def load(source, first, slot, k, sem):
        return pltpu.make_async_copy(
            source.at[pl.ds(pl.multiple_of(first + k * chunk, chunk), chunk)], held.at[slot, k], sem)

    loads = {}
    for k in range(parts):
        loads[IMG, k] = load(image, 0, IMG, k, load_sem.at[0, k])
        loads[IMG, k].start()
    for j in (2, 0, 1, 3):
        for k in range(parts):
            loads[TXT + j, k] = load(text, quarter[j] * rows, TXT + j, k, load_sem.at[1 + j, k])
            loads[TXT + j, k].start()
    own_text = pltpu.make_async_copy(text.at[pl.ds(pl.multiple_of(row * rows, rows), rows)], raw.at[0], raw_sem.at[0])
    own_image = pltpu.make_async_copy(image, raw.at[1], raw_sem.at[1])
    own_text.start()
    own_image.start()

    temp = jnp.exp(jnp.full((8, 128), log_temp[0], jnp.float32))[0:1, 0:1]
    shift = bias[0]

    def normalise(slot, k):
        loads[slot, k].wait()
        for first in range(0, chunk, 64):
            block = pl.ds(first, min(64, chunk))
            full = held[slot, k, block].astype(jnp.float32)
            inverse = lax.rsqrt(jnp.sum(full * full, axis=-1, keepdims=True) + 1e-06)
            held[slot, k, block] = (full * inverse).astype(jnp.bfloat16)

    def copy(kind, k, source, target, device):
        return pltpu.make_async_remote_copy(
            src_ref=held.at[source, k], dst_ref=held.at[target, k],
            send_sem=send_sem.at[kind, k], recv_sem=recv_sem.at[kind, k],
            device_id=device, device_id_type=MESH)

    def x_img(k):
        return copy(X_IMG, k, IMG, IMG + 2, (dp, opposite))

    def c_img(k):
        return copy(C_IMG, k, IMG, IMG + 1, (dp, side))

    def z_img(k):
        return copy(Z_IMG, k, IMG, IMG_NEXT, (down, row))

    def z_img_opp(k):
        return copy(Z_IMG_OPP, k, jnp.where(first_z, IMG, IMG + 2), IMG_NEXT + 2,
                    (down, jnp.where(first_z, opposite, row)))

    def z_txt(k):
        return copy(Z_TXT, k, TXT, TXT_PREV, (up, row))

    def z_txt_opp(k):
        return copy(Z_TXT_OPP, k, jnp.where(last_z, TXT, TXT + 2), TXT_PREV + 2,
                    (up, jnp.where(last_z, opposite, row)))

    def forward(kind, slot):
        return lambda k: copy(kind, k, slot, slot + 1, (dp, side))

    f_img, f_next = forward(F_IMG, IMG + 2), forward(F_NEXT, IMG_NEXT)
    f_next_opp, f_prev_opp = forward(F_NEXT_OPP, IMG_NEXT + 2), forward(F_PREV_OPP, TXT_PREV + 2)
    f_prev = forward(F_PREV, TXT_PREV)

    for k in range(parts):
        normalise(IMG, k)
    pl.semaphore_wait(barrier, len(greeted))
    for k in range(parts):
        x_img(k).start()
        z_img(k).start()
        c_img(k).start()
    for k in range(parts):
        normalise(TXT, k)
        normalise(TXT + 2, k)
        z_txt_opp(k).start()
    for j in (1, 3):
        for k in range(parts):
            normalise(TXT + j, k)

    mine = positive[:, pl.ds(pl.multiple_of(row * rows, 128), rows)]
    pos_cols[...] = jnp.transpose(jnp.broadcast_to(mine, (128, rows)))
    sums[...] = jnp.zeros_like(sums)
    grad_text[...] = jnp.zeros_like(grad_text)
    grad_image[...] = jnp.zeros_like(grad_image)

    def meet(own, slot, k, total, label, with_sums):
        other = held[slot, k]
        cosines[...] = lax.dot_general(
            held[own].reshape(rows, width), other, NT, preferred_element_type=jnp.float32)
        step = min(64, rows)
        for first in range(0, rows, step):
            block = pl.ds(first, step)
            cosine = cosines[block]
            logits = temp * cosine + shift
            if label is not None:
                is_pair = label(first, step)
                logits = jnp.where(is_pair, -logits, logits)
            small = jnp.exp(-jnp.abs(logits))
            upper = 1.0 / (1.0 + small)
            slope = jnp.where(logits >= 0, upper, small * upper)
            if label is not None:
                slope = jnp.where(is_pair, -slope, slope)
            slopes[block] = slope.astype(jnp.bfloat16)
            if with_sums:
                pair_loss = jnp.maximum(logits, 0.0) + jnp.log1p(small)
                for i, value in enumerate((pair_loss, slope * cosine, slope)):
                    value = jnp.sum(value.reshape(step // 8, 8, chunk), axis=0)
                    for lane in range(0, chunk, 128):
                        sums[i * 8:(i + 1) * 8] += value[:, lane:lane + 128]
        total[...] += jnp.dot(slopes[...], other, preferred_element_type=jnp.float32)

    def text_meets(slot, k, base, with_sums=True):
        def label(first, step):
            at = base + k * chunk + lax.broadcasted_iota(jnp.int32, (step, chunk), 1)
            pos = pos_cols[pl.ds(first, step)]
            return jnp.concatenate([pos] * (chunk // 128), axis=1) == at
        meet(TXT, slot, k, grad_text, None if base is None else label, with_sums)

    def image_meets(slot, k, base, with_sums=False):
        if base is not None:
            pos = positive[:, pl.ds(pl.multiple_of(base + k * chunk, 128), chunk)]

        def label(first, step):
            at = row * rows + first + lax.broadcasted_iota(jnp.int32, (step, chunk), 0)
            return jnp.broadcast_to(pos, (step, chunk)) == at
        meet(IMG, slot, k, grad_image, None if base is None else label, with_sums)

    def loop(count, body):
        pl.loop(0, count)(body)

    def exchange(step):
        return pltpu.make_async_remote_copy(
            src_ref=step_out.at[step], dst_ref=step_in.at[step],
            send_sem=step_send.at[step], recv_sem=step_recv.at[step],
            device_id=partners[step], device_id_type=MESH)

    loop(parts, lambda k: text_meets(IMG, k, row * rows))
    for j in range(4):
        loop(parts, lambda k: image_meets(TXT + j, k, quarter[j] * rows))

    @pl.loop(0, parts)
    def _(k):
        c_img(k).wait_recv()
        text_meets(IMG + 1, k, side * rows)

    @pl.loop(0, parts)
    def _(k):
        x_img(k).wait_recv()
        f_img(k).start()
        z_img_opp(k).start()
        text_meets(IMG + 2, k, opposite * rows)
        z_img(k).wait_recv()
        f_next(k).start()
        z_txt_opp(k).wait_recv()
        f_prev_opp(k).start()
        z_txt_opp(k).wait_send()
        z_txt(k).start()
        text_meets(IMG_NEXT, k, None)
        image_meets(TXT_PREV + 2, k, None, True)
        f_img(k).wait_recv()
        text_meets(IMG + 3, k, quarter[3] * rows)
        f_next(k).wait_recv()
        text_meets(IMG_NEXT + 1, k, None)
        f_prev_opp(k).wait_recv()
        image_meets(TXT_PREV + 3, k, None, True)

    step_out[0] = sums[...]
    for step in range(n_steps):
        exchange(step).start()
        exchange(step).wait_recv()
        total = step_out[step] + step_in[step]
        if step + 1 < n_steps:
            step_out[step + 1] = total
    sums[...] = total

    @pl.loop(0, parts)
    def _(k):
        z_img_opp(k).wait_recv()
        f_next_opp(k).start()
        z_txt(k).wait_recv()
        f_prev(k).start()
        text_meets(IMG_NEXT + 2, k, None, False)
        image_meets(TXT_PREV, k, None)
        f_next_opp(k).wait_recv()
        text_meets(IMG_NEXT + 3, k, None, False)
        f_prev(k).wait_recv()
        image_meets(TXT_PREV + 1, k, None)

    own_text.wait()
    own_image.wait()
    for total, which in ((grad_text, 0), (grad_image, 1)):
        @pl.loop(0, rows // 32)
        def _(i):
            block = pl.ds(pl.multiple_of(i * 32, 32), 32)
            full = raw[which, block].astype(jnp.float32)
            inverse = lax.rsqrt(jnp.sum(full * full, axis=-1, keepdims=True) + 1e-06)
            unit = full * inverse
            grad = temp * total[block]
            along = jnp.sum(unit * grad, axis=-1, keepdims=True)
            total[block] = (grad - unit * along) * inverse

    count = rows * 4 * n_dp
    out_sums[0] = jnp.sum(sums[0:8]) / count
    out_sums[1] = jnp.sum(temp * sums[8:16]) / count
    out_sums[2] = jnp.sum(sums[16:24]) / count

    @pl.loop(0, parts)
    def _(k):
        for made in (x_img, c_img, z_img, z_img_opp, z_txt, f_img, f_next, f_next_opp, f_prev_opp, f_prev):
            made(k).wait_send()
    for step in range(n_steps):
        exchange(step).wait_send()


def on_device(n_dp, text, image, positive, log_temp, bias):
    rows, width = image.shape
    chunk = min(256, rows // 2)
    parts = rows // chunk
    n_steps = 2 + (n_dp - 1).bit_length()
    vmem, smem, hbm = (pl.BlockSpec(memory_space=m) for m in (pltpu.VMEM, pltpu.SMEM, pl.ANY))
    dma = pltpu.SemaphoreType.DMA
    grad_text, grad_image, totals = pl.pallas_call(
        functools.partial(kernel, n_dp),
        out_shape=(
            jax.ShapeDtypeStruct((rows, width), jnp.float32),
            jax.ShapeDtypeStruct((rows, width), jnp.float32),
            jax.ShapeDtypeStruct((3,), jnp.float32),
        ),
        in_specs=[hbm, hbm, vmem, smem, smem],
        out_specs=(vmem, vmem, smem),
        scratch_shapes=[
            pltpu.VMEM((16, parts, chunk, width), jnp.bfloat16),
            pltpu.VMEM((2, rows, width), jnp.bfloat16),
            pltpu.VMEM((rows, chunk), jnp.float32),
            pltpu.VMEM((rows, chunk), jnp.bfloat16),
            pltpu.VMEM((rows, 128), jnp.int32),
            pltpu.VMEM((24, 128), jnp.float32),
            pltpu.VMEM((n_steps, 24, 128), jnp.float32),
            pltpu.VMEM((n_steps, 24, 128), jnp.float32),
            dma((5, parts)), dma((2,)), dma((11, parts)), dma((11, parts)), dma((n_steps,)), dma((n_steps,)),
        ],
        compiler_params=pltpu.CompilerParams(
            collective_id=0, has_side_effects=True, vmem_limit_bytes=48 * 1024 * 1024),
        cost_estimate=pl.CostEstimate(
            flops=2 * 32 * rows * rows * width, bytes_accessed=7 * rows * width * 2 + 2 * rows * width * 4,
            transcendentals=24 * rows * rows),
    )(text, image, positive, log_temp, bias)
    return grad_text, grad_image, totals[0:1], totals[1:2], totals[2:3]


def solution(mesh):
    return jax.shard_map(
        functools.partial(on_device, mesh.shape["dp"]),
        mesh=mesh,
        in_specs=(P("dp", None), P(("dp", "row"), None), P("dp", None), P(), P()),
        out_specs=(P(("dp", "row"), None), P(("dp", "row"), None), P(), P(), P()),
        check_vma=False,
    )
```

```python
import functools

import jax
import jax.numpy as jnp
from jax import lax
from jax.experimental import pallas as pl
from jax.experimental.pallas import tpu as pltpu
from jax.sharding import PartitionSpec as P

MESH = pl.DeviceIdType.MESH
NT = (((1,), (1,)), ((), ()))
LANES = 128

IMG, NEXT, TXT, PREV = range(4)

X_IMG, C_IMG, F_IMG, Z_IMG, F_NEXT, Z_TXT, F_PREV = 0, 1, 2, 3, 5, 7, 9
KINDS = 11
FOR_SIDE = 11
X_NEXT = 14


def kernel(n_dp, text, image, positive, log_temp, bias, grad_text, grad_image, out_sums,
           held, raw, cosines, slopes, pos, pos_cols, pos_rows, sums, met_a, met_b,
           load_sem, raw_sem, send_sem, recv_sem, send_a, recv_a, send_b, recv_b):
    parts, width = held.shape[2], held.shape[-1]
    rows = parts * LANES
    dp, row = lax.axis_index("dp"), lax.axis_index("row")
    side = row + 1 - 2 * (row % 2)
    opposite = (row + 2) % 4
    quarter = ((row, side), (opposite, (side + 2) % 4))
    up, down = (dp + 1) % n_dp, (dp + n_dp - 1) % n_dp
    first_z, last_z = dp % 4 == 0, dp % 4 == 3
    end_z = jnp.logical_or(first_z, last_z)
    before_last_z = dp % 4 == 2
    core0, core1 = row % 2 == 0, row % 2 == 1
    opposite_side = quarter[1][1]

    n_b = met_b.shape[0]
    n_y = n_dp // n_b
    y, rest = dp // n_b, dp % n_b
    place_a = y * 4 + row
    group_a = [(((y + i // 4) % n_y) * n_b + rest, (row + i % 4) % 4) for i in range(1, 4 * n_y)]
    group_b = [(y * n_b + (rest + i) % n_b, row) for i in range(1, n_b)]

    barrier = pltpu.get_barrier_semaphore()
    greeted = [(near, (row + i) % 4) for near in (up, down) for i in range(4)] + group_a + group_b
    for device in greeted:
        pl.semaphore_signal(barrier, inc=1, device_id=device, device_id_type=MESH)

    def load(source, first, group, pair, k, core):
        first = pl.multiple_of(first + k * LANES, LANES)
        return pltpu.make_async_copy(source.at[pl.ds(first, LANES)], held.at[group, pair, k, core],
                                     load_sem.at[0 if group == IMG else 1 + 2 * pair + core, k])

    def load_image(k):
        return load(image, 0, IMG, 0, k, 0)

    def load_text(pair, core, k):
        return load(text, quarter[pair][core] * rows, TXT, pair, k, core)

    for k in range(parts):
        load_image(k).start()
    pos_copy = pltpu.make_async_copy(positive, pos, raw_sem.at[2])
    for pair, core in ((0, 0), (1, 0), (0, 1), (1, 1)):
        for k in range(parts):
            load_text(pair, core, k).start()
        if core == 0 and pair == 1:
            pos_copy.start()
    own_text = pltpu.make_async_copy(text.at[pl.ds(pl.multiple_of(row * rows, rows), rows)], raw.at[0], raw_sem.at[0])
    own_image = pltpu.make_async_copy(image, raw.at[1], raw_sem.at[1])
    own_text.start()
    own_image.start()

    temp = jnp.exp(jnp.full((8, LANES), log_temp[0], jnp.float32))[0:1, 0:1]
    shift = bias[0]

    def normalise(group, pair, k, core):
        full = held[group, pair, k, core].astype(jnp.float32)
        inverse = lax.rsqrt(jnp.sum(full * full, axis=-1, keepdims=True) + 1e-06)
        held[group, pair, k, core] = (full * inverse).astype(jnp.bfloat16)

    def copy(kind, k, source, target, device, sent=None):
        return pltpu.make_async_remote_copy(
            src_ref=held.at[source], dst_ref=held.at[target],
            send_sem=send_sem.at[kind if sent is None else sent, k], recv_sem=recv_sem.at[kind, k],
            device_id=device, device_id_type=MESH)

    def x_img(k):
        return copy(X_IMG, k, (IMG, 0, k, 0), (IMG, 1, k, 0), (dp, opposite))

    def x_img_for_side(k):
        return copy(X_IMG, k, (IMG, 0, k, 1), (IMG, 1, k, 0), (dp, opposite_side), FOR_SIDE)

    def c_img(k):
        return copy(C_IMG, k, (IMG, 0, k, 0), (IMG, 0, k, 1), (dp, side))

    def f_img(k):
        return copy(F_IMG, k, (IMG, 1, k, 0), (IMG, 1, k, 1), (dp, side))

    def z_img(pair, k):
        across = jnp.logical_and(first_z, pair == 1)
        return copy(Z_IMG + pair, k, (IMG, jnp.where(across, 0, pair), k, 0), (NEXT, pair, k, 0),
                    (down, jnp.where(across, opposite, row)))

    def x_next(k):
        return copy(Z_IMG + 1, k, (NEXT, 0, k, 0), (NEXT, 1, k, 0), (dp, opposite), X_NEXT)

    def z_img_for_side(pair, k):
        return copy(Z_IMG + pair, k, (IMG, 0, k, 1), (NEXT, pair, k, 0),
                    (down, opposite_side if pair else side), FOR_SIDE + 1 + pair)

    def z_txt(pair, k):
        across = jnp.logical_and(last_z, pair == 1)
        return copy(Z_TXT + pair, k, (TXT, jnp.where(across, 0, pair), k, 0), (PREV, pair, k, 0),
                    (up, jnp.where(across, opposite, row)))

    def z_txt_for_side(pair, k):
        return copy(Z_TXT + pair, k, (TXT, 0, k, 1), (PREV, pair, k, 0),
                    (up, opposite_side if pair else side), FOR_SIDE + 1 + pair)

    def f_next(pair, k):
        return copy(F_NEXT + pair, k, (NEXT, pair, k, 0), (NEXT, pair, k, 1), (dp, side))

    def f_prev(pair, k):
        return copy(F_PREV + pair, k, (PREV, pair, k, 0), (PREV, pair, k, 1), (dp, side))

    sends_x = jnp.logical_or(jnp.logical_not(end_z), core1)
    sends_img = jnp.logical_or(jnp.logical_not(first_z), core0)
    sends_txt = jnp.logical_or(jnp.logical_not(last_z), core0)
    img_for_side = jnp.logical_and(first_z, core0)
    txt_for_side = jnp.logical_and(last_z, core0)
    x_for_side = jnp.logical_and(end_z, core1)

    for k in range(parts):
        load_image(k).wait()
        normalise(IMG, 0, k, 0)
        if k == 0:
            pl.semaphore_wait(barrier, len(greeted))
        c_img(k).start()

        @pl.when(jnp.logical_not(end_z))
        def _():
            x_img(k).start()
            z_img(0, k).start()

    for k in range(parts):
        c_img(k).wait_recv()

        @pl.when(jnp.logical_and(end_z, core1))
        def _():
            x_img(k).start()
            x_img_for_side(k).start()

        @pl.when(last_z)
        def _():
            z_img(0, k).start()

        @pl.when(img_for_side)
        def _():
            z_img(0, k).start()
            z_img(1, k).start()
            z_img_for_side(0, k).start()
            z_img_for_side(1, k).start()

    for k in range(parts):
        load_text(0, 0, k).wait()
        normalise(TXT, 0, k, 0)

        @pl.when(sends_txt)
        def _():
            z_txt(0, k).start()

        load_text(0, 1, k).wait()
        normalise(TXT, 0, k, 1)

        @pl.when(txt_for_side)
        def _():
            z_txt(1, k).start()
            z_txt_for_side(0, k).start()
            z_txt_for_side(1, k).start()

    for k in range(parts):
        load_text(1, 0, k).wait()
        normalise(TXT, 1, k, 0)

        @pl.when(jnp.logical_not(last_z))
        def _():
            z_txt(1, k).start()

    for k in range(parts):
        load_text(1, 1, k).wait()
        normalise(TXT, 1, k, 1)

    pos_copy.wait()
    mine = pos[:, pl.ds(pl.multiple_of(row * rows, LANES), rows)]
    pos_cols[...] = jnp.transpose(jnp.broadcast_to(mine, (LANES, rows)))
    for pair in range(2):
        for k in range(parts):
            for core in range(2):
                at = pl.multiple_of(quarter[pair][core] * rows + k * LANES, LANES)
                pos_rows[pair, :, pl.ds((2 * k + core) * LANES, LANES)] = pos[:, pl.ds(at, LANES)]
    sums[...] = jnp.zeros_like(sums)

    span = 2 * LANES
    step = 64

    def meet(own, group, pair, k0, count, total, label, with_sums, fresh=False):
        mine = held[own, 0, :, 0].reshape(rows, width)
        for i in range(count):
            other = held[group, pair, k0 + i].reshape(span, width)
            here = cosines.at[i % 2]
            here[...] = lax.dot_general(mine, other, NT, preferred_element_type=jnp.float32)
            for first in range(0, rows, step):
                block = pl.ds(first, step)
                cosine = here[block]
                logits = temp * cosine + shift
                if label is not None:
                    is_pair = label(first, k0 + i)
                    logits = jnp.where(is_pair, -logits, logits)
                small = jnp.exp(-jnp.abs(logits))
                upper = 1.0 / (1.0 + small)
                slope = jnp.where(logits >= 0, upper, small * upper)
                if label is not None:
                    slope = jnp.where(is_pair, -slope, slope)
                slopes[block, i * span:(i + 1) * span] = slope.astype(jnp.bfloat16)
                if with_sums:
                    pair_loss = jnp.maximum(logits, 0.0) + jnp.log1p(small)
                    for j, value in enumerate((pair_loss, slope * cosine, slope)):
                        value = jnp.sum(value.reshape(step // 8, 8, span), axis=0)
                        sums[j * 8:(j + 1) * 8] += value[:, :LANES] + value[:, LANES:]
        product = jnp.dot(slopes[:, :count * span], held[group, pair, pl.ds(k0, count)].reshape(count * span, width),
                          preferred_element_type=jnp.float32)
        total[...] = product if fresh else total[...] + product

    def text_meets_own(pair, k0, count, fresh=False):
        def label(first, k):
            lane = lax.broadcasted_iota(jnp.int32, (step, LANES), 1) + k * LANES
            at = jnp.concatenate([lane + quarter[pair][core] * rows for core in range(2)], axis=1)
            here = pos_cols[pl.ds(first, step)]
            return jnp.concatenate([here, here], axis=1) == at
        meet(TXT, IMG, pair, k0, count, grad_text, label, True, fresh)

    def image_meets_own(pair, fresh=False):
        def label(first, k):
            at = lax.broadcasted_iota(jnp.int32, (step, span), 0) + (row * rows + first)
            return jnp.broadcast_to(pos_rows[pair, :, pl.ds(k * span, span)], (step, span)) == at
        meet(IMG, TXT, pair, 0, parts, grad_image, label, False, fresh)

    image_meets_own(0, True)
    text_meets_own(0, 0, parts, True)
    image_meets_own(1)

    def to_a(i):
        return pltpu.make_async_remote_copy(
            src_ref=sums, dst_ref=met_a.at[place_a], send_sem=send_a.at[i], recv_sem=recv_a.at[i],
            device_id=group_a[i], device_id_type=MESH)

    def to_b(i):
        return pltpu.make_async_remote_copy(
            src_ref=met_b.at[rest], dst_ref=met_b.at[rest], send_sem=send_b.at[i], recv_sem=recv_b.at[i],
            device_id=group_b[i], device_id_type=MESH)

    @pl.loop(0, 2 * parts)
    def _(s):
        next_pair, next_k = jnp.where(last_z, s % 2, s // parts), jnp.where(last_z, s // 2, s % parts)
        prev_pair, prev_k = jnp.where(first_z, s % 2, s // parts), jnp.where(first_z, s // 2, s % parts)
        x_now = jnp.where(end_z, s % 2, 1 - s // parts) == 1
        x_k = jnp.where(end_z, s // 2, s % parts)

        @pl.when(x_now)
        def _():
            x_img(x_k).wait_recv()
            f_img(x_k).start()

            @pl.when(jnp.logical_not(end_z))
            def _():
                z_img(1, x_k).start()

        z_img(next_pair, next_k).wait_recv()
        f_next(next_pair, next_k).start()

        @pl.when(jnp.logical_and(before_last_z, s < parts))
        def _():
            x_next(next_k).start()

        z_txt(prev_pair, prev_k).wait_recv()
        f_prev(prev_pair, prev_k).start()
        f_next(next_pair, next_k).wait_recv()
        meet(TXT, NEXT, next_pair, next_k, 1, grad_text, None, True)

        @pl.when(x_now)
        def _():
            f_img(x_k).wait_recv()
            text_meets_own(1, x_k, 1)

        @pl.when(s == 2 * parts - 1)
        def _():
            for i in range(len(group_a)):
                to_a(i).start()
            met_a[place_a] = sums[...]

        f_prev(prev_pair, prev_k).wait_recv()
        meet(IMG, PREV, prev_pair, prev_k, 1, grad_image, None, False)

    for i in range(len(group_a)):
        to_a(i).wait_recv()
    met_b[rest] = functools.reduce(lambda a, b: a + b, [met_a[i] for i in range(4 * n_y)])
    for i in range(len(group_b)):
        to_b(i).start()

    own_text.wait()
    own_image.wait()
    for total, which in ((grad_text, 0), (grad_image, 1)):
        @pl.loop(0, parts)
        def _(k):
            block = pl.ds(pl.multiple_of(k * LANES, LANES), LANES)
            full = raw[which, block].astype(jnp.float32)
            grad = temp * total[block]
            inverse = lax.rsqrt(jnp.sum(full * full, axis=-1, keepdims=True) + 1e-06)
            unit = full * inverse
            along = jnp.sum(unit * grad, axis=-1, keepdims=True)
            total[block] = (grad - unit * along) * inverse

    for i in range(len(group_b)):
        to_b(i).wait_recv()
    total = functools.reduce(lambda a, b: a + b, [met_b[i] for i in range(n_b)])
    count = rows * 4 * n_dp
    out_sums[0] = jnp.sum(total[0:8]) / count
    out_sums[1] = jnp.sum(temp * total[8:16]) / count
    out_sums[2] = jnp.sum(total[16:24]) / count

    @pl.loop(0, parts)
    def _(k):
        for made in (c_img, f_img):
            made(k).wait_send()
        for pair in range(2):
            for made in (f_next, f_prev):
                made(pair, k).wait_send()

        @pl.when(sends_x)
        def _():
            x_img(k).wait_send()

        @pl.when(x_for_side)
        def _():
            x_img_for_side(k).wait_send()

        @pl.when(before_last_z)
        def _():
            x_next(k).wait_send()

        for sends, for_side, made, made_for_side in (
                (sends_img, img_for_side, z_img, z_img_for_side), (sends_txt, txt_for_side, z_txt, z_txt_for_side)):
            @pl.when(sends)
            def _():
                made(0, k).wait_send()

            @pl.when(jnp.logical_and(sends, jnp.logical_not(last_z)) if made is z_img else sends)
            def _():
                made(1, k).wait_send()

            @pl.when(for_side)
            def _():
                for pair in range(2):
                    made_for_side(pair, k).wait_send()

    for i in range(len(group_a)):
        to_a(i).wait_send()
    for i in range(len(group_b)):
        to_b(i).wait_send()


def on_device(n_dp, text, image, positive, log_temp, bias):
    rows, width = image.shape
    parts = rows // LANES
    n_b = min(n_dp, 8)
    n_a = 4 * (n_dp // n_b)
    vmem, smem, hbm = (pl.BlockSpec(memory_space=m) for m in (pltpu.VMEM, pltpu.SMEM, pltpu.HBM))
    dma = pltpu.SemaphoreType.DMA
    grad_text, grad_image, totals = pl.pallas_call(
        functools.partial(kernel, n_dp),
        out_shape=(
            jax.ShapeDtypeStruct((rows, width), jnp.float32),
            jax.ShapeDtypeStruct((rows, width), jnp.float32),
            jax.ShapeDtypeStruct((3,), jnp.float32),
        ),
        in_specs=[hbm, hbm, hbm, smem, smem],
        out_specs=(vmem, vmem, smem),
        scratch_shapes=[
            pltpu.VMEM((4, 2, parts, 2, LANES, width), jnp.bfloat16),
            pltpu.VMEM((2, rows, width), jnp.bfloat16),
            pltpu.VMEM((2, rows, 2 * LANES), jnp.float32),
            pltpu.VMEM((rows, 2 * rows), jnp.bfloat16),
            pltpu.VMEM((1, 4 * rows), jnp.int32),
            pltpu.VMEM((rows, LANES), jnp.int32),
            pltpu.VMEM((2, 1, 2 * rows), jnp.int32),
            pltpu.VMEM((24, LANES), jnp.float32),
            pltpu.VMEM((n_a, 24, LANES), jnp.float32),
            pltpu.VMEM((n_b, 24, LANES), jnp.float32),
            dma((5, parts)), dma((3,)), dma((KINDS + 4, parts)), dma((KINDS, parts)),
            dma((n_a,)), dma((n_a,)), dma((n_b,)), dma((n_b,)),
        ],
        compiler_params=pltpu.CompilerParams(
            collective_id=0, has_side_effects=True, vmem_limit_bytes=48 * 1024 * 1024),
        cost_estimate=pl.CostEstimate(
            flops=2 * 32 * rows * rows * width, bytes_accessed=7 * rows * width * 2 + 2 * rows * width * 4,
            transcendentals=24 * rows * rows),
    )(text, image, positive, log_temp, bias)
    return grad_text, grad_image, totals[0:1], totals[1:2], totals[2:3]


def solution(mesh):
    return jax.shard_map(
        functools.partial(on_device, mesh.shape["dp"]),
        mesh=mesh,
        in_specs=(P("dp", None), P(("dp", "row"), None), P("dp", None), P(), P()),
        out_specs=(P(("dp", "row"), None), P(("dp", "row"), None), P(), P(), P()),
        check_vma=False,
    )
```

```python
import functools

import jax
import jax.numpy as jnp
from jax import lax
from jax.experimental import pallas as pl
from jax.experimental.pallas import tpu as pltpu
from jax.sharding import PartitionSpec as P

MESH = pl.DeviceIdType.MESH
NT = (((1,), (1,)), ((), ()))
LANES = 128

IMG, NEXT, TXT, PREV = range(4)

X_IMG, C_IMG, F_IMG, Z_IMG, F_NEXT, Z_TXT, F_PREV = 0, 1, 2, 3, 5, 7, 9
KINDS = 11
FOR_SIDE = 11
X_NEXT = 14


def kernel(n_dp, text, image, positive, log_temp, bias, grad_text, grad_image, out_sums,
           held, raw, inverses, cosines, slopes, pos, pos_cols, pos_rows, sums, packed, met_a, met_b,
           load_sem, raw_sem, send_sem, recv_sem, send_a, recv_a, send_b, recv_b):
    parts, width = held.shape[2], held.shape[-1]
    rows = parts * LANES
    dp, row = lax.axis_index("dp"), lax.axis_index("row")
    side = row + 1 - 2 * (row % 2)
    opposite = (row + 2) % 4
    quarter = ((row, side), (opposite, (side + 2) % 4))
    up, down = (dp + 1) % n_dp, (dp + n_dp - 1) % n_dp
    first_z, last_z = dp % 4 == 0, dp % 4 == 3
    end_z = jnp.logical_or(first_z, last_z)
    before_last_z = dp % 4 == 2
    core0, core1 = row % 2 == 0, row % 2 == 1
    opposite_side = quarter[1][1]

    n_b = met_b.shape[0]
    n_y = n_dp // n_b
    y, rest = dp // n_b, dp % n_b
    place_a = y * 4 + row
    group_a = [(((y + i // 4) % n_y) * n_b + rest, (row + i % 4) % 4) for i in range(1, 4 * n_y)]
    group_b = [(y * n_b + (rest + i) % n_b, row) for i in range(1, n_b)]

    barrier = pltpu.get_barrier_semaphore()
    greeted = [(near, (row + i) % 4) for near in (up, down) for i in range(4)] + group_a + group_b
    for device in greeted:
        pl.semaphore_signal(barrier, inc=1, device_id=device, device_id_type=MESH)

    def load(source, first, group, pair, k, core):
        first = pl.multiple_of(first + k * LANES, LANES)
        return pltpu.make_async_copy(source.at[pl.ds(first, LANES)], held.at[group, pair, k, core],
                                     load_sem.at[0 if group == IMG else 1 + 2 * pair + core, k])

    def load_image(k):
        return load(image, 0, IMG, 0, k, 0)

    def load_text(pair, core, k):
        return load(text, quarter[pair][core] * rows, TXT, pair, k, core)

    for k in range(parts):
        load_image(k).start()
    pos_copy = pltpu.make_async_copy(positive, pos, raw_sem.at[2])
    for pair, core in ((0, 0), (1, 0), (0, 1), (1, 1)):
        for k in range(parts):
            load_text(pair, core, k).start()
        if core == 0 and pair == 1:
            pos_copy.start()
    own_text = pltpu.make_async_copy(text.at[pl.ds(pl.multiple_of(row * rows, rows), rows)], raw.at[0], raw_sem.at[0])
    own_image = pltpu.make_async_copy(image, raw.at[1], raw_sem.at[1])
    own_text.start()
    own_image.start()

    temp = jnp.exp(jnp.full((8, LANES), log_temp[0], jnp.float32))[0:1, 0:1]
    shift = bias[0]

    def normalise(group, pair, k, core):
        full = held[group, pair, k, core].astype(jnp.float32)
        inverse = lax.rsqrt(jnp.sum(full * full, axis=-1, keepdims=True) + 1e-06)
        held[group, pair, k, core] = (full * inverse).astype(jnp.bfloat16)
        if pair == 0 and core == 0:
            inverses[0 if group == TXT else 1, k] = jnp.broadcast_to(inverse, (LANES, LANES))

    def copy(kind, k, source, target, device, sent=None):
        return pltpu.make_async_remote_copy(
            src_ref=held.at[source], dst_ref=held.at[target],
            send_sem=send_sem.at[kind if sent is None else sent], recv_sem=recv_sem.at[kind, k],
            device_id=device, device_id_type=MESH)

    def x_img(k):
        return copy(X_IMG, k, (IMG, 0, k, 0), (IMG, 1, k, 0), (dp, opposite))

    def x_img_for_side(k):
        return copy(X_IMG, k, (IMG, 0, k, 1), (IMG, 1, k, 0), (dp, opposite_side), FOR_SIDE)

    def c_img(k):
        return copy(C_IMG, k, (IMG, 0, k, 0), (IMG, 0, k, 1), (dp, side))

    def f_img(k):
        return copy(F_IMG, k, (IMG, 1, k, 0), (IMG, 1, k, 1), (dp, side))

    def z_img(pair, k):
        across = jnp.logical_and(first_z, pair == 1)
        return copy(Z_IMG + pair, k, (IMG, jnp.where(across, 0, pair), k, 0), (NEXT, pair, k, 0),
                    (down, jnp.where(across, opposite, row)))

    def x_next(k):
        return copy(Z_IMG + 1, k, (NEXT, 0, k, 0), (NEXT, 1, k, 0), (dp, opposite), X_NEXT)

    def z_img_for_side(pair, k):
        return copy(Z_IMG + pair, k, (IMG, 0, k, 1), (NEXT, pair, k, 0),
                    (down, opposite_side if pair else side), FOR_SIDE + 1 + pair)

    def z_txt(pair, k):
        across = jnp.logical_and(last_z, pair == 1)
        return copy(Z_TXT + pair, k, (TXT, jnp.where(across, 0, pair), k, 0), (PREV, pair, k, 0),
                    (up, jnp.where(across, opposite, row)))

    def z_txt_for_side(pair, k):
        return copy(Z_TXT + pair, k, (TXT, 0, k, 1), (PREV, pair, k, 0),
                    (up, opposite_side if pair else side), FOR_SIDE + 1 + pair)

    def f_next(pair, k):
        return copy(F_NEXT + pair, k, (NEXT, pair, k, 0), (NEXT, pair, k, 1), (dp, side))

    def f_prev(pair, k):
        return copy(F_PREV + pair, k, (PREV, pair, k, 0), (PREV, pair, k, 1), (dp, side))

    sends_x = jnp.logical_or(jnp.logical_not(end_z), core1)
    sends_img = jnp.logical_or(jnp.logical_not(first_z), core0)
    sends_txt = jnp.logical_or(jnp.logical_not(last_z), core0)
    img_for_side = jnp.logical_and(first_z, core0)
    txt_for_side = jnp.logical_and(last_z, core0)
    x_for_side = jnp.logical_and(end_z, core1)

    for k in range(parts):
        load_image(k).wait()
        normalise(IMG, 0, k, 0)
        if k == 0:
            pl.semaphore_wait(barrier, len(greeted))
        c_img(k).start()

        @pl.when(jnp.logical_not(end_z))
        def _():
            x_img(k).start()

        @pl.when(jnp.logical_not(first_z))
        def _():
            z_img(0, k).start()

        if k == 0:
            @pl.when(img_for_side)
            def _():
                z_img(0, k).start()
                z_img(1, k).start()

            @pl.when(x_for_side)
            def _():
                x_img(k).start()

    for k in range(parts):
        load_text(0, 0, k).wait()
        normalise(TXT, 0, k, 0)

        @pl.when(sends_txt)
        def _():
            z_txt(0, k).start()

        load_text(0, 1, k).wait()
        normalise(TXT, 0, k, 1)

        @pl.when(txt_for_side)
        def _():
            z_txt(1, k).start()
            z_txt_for_side(0, k).start()
            z_txt_for_side(1, k).start()

        c_img(k).wait_recv()

        @pl.when(x_for_side)
        def _():
            x_img_for_side(k).start()
            if k + 1 < parts:
                x_img(k + 1).start()

        @pl.when(img_for_side)
        def _():
            z_img_for_side(0, k).start()
            z_img_for_side(1, k).start()
            if k + 1 < parts:
                z_img(0, k + 1).start()
                z_img(1, k + 1).start()

    for k in range(parts):
        load_text(1, 0, k).wait()
        normalise(TXT, 1, k, 0)

        @pl.when(jnp.logical_not(last_z))
        def _():
            z_txt(1, k).start()

    for k in range(parts):
        load_text(1, 1, k).wait()
        normalise(TXT, 1, k, 1)

    pos_copy.wait()
    mine = pos[:, pl.ds(pl.multiple_of(row * rows, LANES), rows)]
    pos_cols[...] = jnp.transpose(jnp.broadcast_to(mine, (LANES, rows)))
    for pair in range(2):
        for k in range(parts):
            for core in range(2):
                at = pl.multiple_of(quarter[pair][core] * rows + k * LANES, LANES)
                pos_rows[pair, :, pl.ds((2 * k + core) * LANES, LANES)] = pos[:, pl.ds(at, LANES)]
    sums[...] = jnp.zeros_like(sums)

    span = 2 * LANES
    step = 64

    def meet(own, group, pieces, total, label, with_sums, joined=True, fresh=False, between=None):
        mine = held[own, 0, :, 0].reshape(rows, width)
        for i, (pair, k) in enumerate(pieces):
            other = held[group, pair, k].reshape(span, width)
            here = cosines.at[i % 2]
            here[...] = lax.dot_general(mine, other, NT, preferred_element_type=jnp.float32)
            for first in range(0, rows, step):
                block = pl.ds(first, step)
                cosine = here[block]
                logits = temp * cosine + shift
                if label is not None:
                    is_pair = label(first, k)
                    logits = jnp.where(is_pair, -logits, logits)
                small = jnp.exp(-jnp.abs(logits))
                upper = 1.0 / (1.0 + small)
                slope = jnp.where(logits >= 0, upper, small * upper)
                if label is not None:
                    slope = jnp.where(is_pair, -slope, slope)
                slopes[block, i * span:(i + 1) * span] = slope.astype(jnp.bfloat16)
                if with_sums:
                    pair_loss = jnp.maximum(logits, 0.0) + jnp.log1p(small)
                    for j, value in enumerate((pair_loss, slope * cosine, slope)):
                        value = jnp.sum(value.reshape(step // 8, 8, span), axis=0)
                        sums[j * 8:(j + 1) * 8] += value[:, :LANES] + value[:, LANES:]
        if between is not None:
            between()
        if joined:
            count = len(pieces)
            (pair, k0) = pieces[0]
            product = jnp.dot(slopes[:, :count * span], held[group, pair, pl.ds(k0, count)].reshape(count * span, width),
                              preferred_element_type=jnp.float32)
            total[...] = product if fresh else total[...] + product
        else:
            total[...] += sum(jnp.dot(slopes[:, i * span:(i + 1) * span], held[group, pair, k].reshape(span, width),
                                      preferred_element_type=jnp.float32) for i, (pair, k) in enumerate(pieces))

    def text_meets_own(pair, k0, count, fresh=False):
        def label(first, k):
            lane = lax.broadcasted_iota(jnp.int32, (step, LANES), 1) + k * LANES
            at = jnp.concatenate([lane + quarter[pair][core] * rows for core in range(2)], axis=1)
            here = pos_cols[pl.ds(first, step)]
            return jnp.concatenate([here, here], axis=1) == at
        meet(TXT, IMG, [(pair, k0 + i) for i in range(count)], grad_text, label, True, fresh=fresh)

    def image_meets_own(pair, fresh=False):
        def label(first, k):
            at = lax.broadcasted_iota(jnp.int32, (step, span), 0) + (row * rows + first)
            return jnp.broadcast_to(pos_rows[pair, :, pl.ds(k * span, span)], (step, span)) == at
        meet(IMG, TXT, [(pair, k) for k in range(parts)], grad_image, label, False, fresh=fresh)

    image_meets_own(0, True)
    text_meets_own(0, 0, parts, True)
    image_meets_own(1)

    def bytes_of(ref, sent, arrived):
        return pltpu.make_async_remote_copy(src_ref=ref, dst_ref=ref, send_sem=sent, recv_sem=arrived,
                                            device_id=(dp, side), device_id_type=MESH)

    def to_a(i):
        return pltpu.make_async_remote_copy(
            src_ref=packed, dst_ref=met_a.at[place_a], send_sem=send_a, recv_sem=recv_a,
            device_id=group_a[i], device_id_type=MESH)

    def to_b(i):
        return pltpu.make_async_remote_copy(
            src_ref=met_b.at[rest], dst_ref=met_b.at[rest], send_sem=send_b, recv_sem=recv_b,
            device_id=group_b[i], device_id_type=MESH)

    def finish(total, which):
        @pl.loop(0, parts)
        def _(k):
            block = pl.ds(pl.multiple_of(k * LANES, LANES), LANES)
            full = raw[which, block].astype(jnp.float32)
            grad = temp * total[block]
            inverse = inverses[which, k][:, 0:1]
            unit = full * inverse
            along = jnp.sum(unit * grad, axis=-1, keepdims=True)
            total[block] = (grad - unit * along) * inverse

    own_text.wait()
    own_image.wait()
    packed[...] = jnp.zeros_like(packed)

    @pl.loop(0, parts)
    def _(t):
        def pieces(together):
            return [(jnp.where(together, s % 2, s // parts), jnp.where(together, s // 2, s % parts))
                    for s in (2 * t, 2 * t + 1)]

        nexts, prevs = pieces(last_z), pieces(first_z)
        early = t < parts // 2
        x_two = jnp.logical_and(jnp.logical_not(end_z), early)

        @pl.when(x_two)
        def _():
            for i in range(2):
                x_img(2 * t + i).wait_recv()
                f_img(2 * t + i).start()
                z_img(1, 2 * t + i).start()

        for i in range(2):
            z_img(*nexts[i]).wait_recv()
            f_next(*nexts[i]).start()

            @pl.when(jnp.logical_and(before_last_z, early))
            def _():
                x_next(nexts[i][1]).start()

            z_txt(*prevs[i]).wait_recv()
            f_prev(*prevs[i]).start()

        @pl.when(end_z)
        def _():
            x_img(t).wait_recv()
            f_img(t).start()

        @pl.when(x_two)
        def _():
            for i in range(2):
                f_img(2 * t + i).wait_recv()
            text_meets_own(1, 2 * t, 2)

        @pl.when(end_z)
        def _():
            f_img(t).wait_recv()
            text_meets_own(1, t, 1)

        last = t == parts - 1

        def start_sums():
            @pl.when(last)
            def _():
                for i in range(3):
                    packed[i:i + 1] = jnp.sum(sums[8 * i:8 * (i + 1)], axis=0, keepdims=True)
                for i in range(len(group_a)):
                    to_a(i).start()

        for i in range(2):
            f_next(*nexts[i]).wait_recv()
        meet(TXT, NEXT, nexts, grad_text, None, True, joined=False, between=start_sums)

        @pl.when(last)
        def _():
            finish(grad_text, 0)
            met_a[place_a] = packed[...]
            bytes_of(met_a.at[pl.ds(0, len(group_a))], send_a, recv_a).wait_recv()
            met_b[rest] = functools.reduce(lambda a, b: a + b, [met_a[i] for i in range(4 * n_y)])
            for i in range(len(group_b)):
                to_b(i).start()

        for i in range(2):
            f_prev(*prevs[i]).wait_recv()
        meet(IMG, PREV, prevs, grad_image, None, False, joined=False)

    finish(grad_image, 1)
    bytes_of(met_b.at[pl.ds(0, len(group_b))], send_b, recv_b).wait_recv()
    total = functools.reduce(lambda a, b: a + b, [met_b[i] for i in range(n_b)])
    count = rows * 4 * n_dp
    out_sums[...] = total / count
    out_sums[1:2] = temp * total[1:2] / count

    def all_sent(*kinds):
        for kind in kinds:
            bytes_of(raw.at[0], send_sem.at[kind], recv_sem.at[0, 0]).wait_send()

    all_sent(C_IMG, F_IMG, F_NEXT, F_NEXT + 1, F_PREV, F_PREV + 1)
    for sends, kinds in ((sends_x, (X_IMG,)), (x_for_side, (FOR_SIDE,)), (before_last_z, (X_NEXT,)),
                         (sends_img, (Z_IMG,)), (jnp.logical_and(sends_img, jnp.logical_not(last_z)), (Z_IMG + 1,)),
                         (img_for_side, (FOR_SIDE + 1, FOR_SIDE + 2)),
                         (sends_txt, (Z_TXT, Z_TXT + 1)), (txt_for_side, (FOR_SIDE + 1, FOR_SIDE + 2))):
        @pl.when(sends)
        def _():
            all_sent(*kinds)

    bytes_of(met_a.at[pl.ds(0, len(group_a))], send_a, recv_a).wait_send()
    bytes_of(met_b.at[pl.ds(0, len(group_b))], send_b, recv_b).wait_send()


def write_out(grad_text, grad_image, sums, out_text, out_image, loss, grad_log_temp, grad_bias, sem):
    half = grad_text.shape[0] // 2
    copies = [pltpu.make_async_copy(source.at[pl.ds(i * half, half)], target.at[pl.ds(i * half, half)], sem.at[2 * j + i])
              for j, (source, target) in enumerate(((grad_text, out_text), (grad_image, out_image))) for i in range(2)]
    for copy in copies:
        copy.start()
    for j, out in enumerate((loss, grad_log_temp, grad_bias)):
        out[0] = jnp.sum(sums[j:j + 1])
    for copy in copies:
        copy.wait()


def on_device(n_dp, text, image, positive, log_temp, bias):
    rows, width = image.shape
    parts = rows // LANES
    n_b = min(n_dp, 8)
    n_a = 4 * (n_dp // n_b)
    vmem, smem, hbm = (pl.BlockSpec(memory_space=m) for m in (pltpu.VMEM, pltpu.SMEM, pltpu.HBM))
    dma = pltpu.SemaphoreType.DMA
    results = pl.pallas_call(
        functools.partial(kernel, n_dp),
        out_shape=(
            jax.ShapeDtypeStruct((rows, width), jnp.float32),
            jax.ShapeDtypeStruct((rows, width), jnp.float32),
            jax.ShapeDtypeStruct((8, LANES), jnp.float32),
        ),
        in_specs=[hbm, hbm, hbm, smem, smem],
        out_specs=(vmem, vmem, vmem),
        scratch_shapes=[
            pltpu.VMEM((4, 2, parts, 2, LANES, width), jnp.bfloat16),
            pltpu.VMEM((2, rows, width), jnp.bfloat16),
            pltpu.VMEM((2, parts, LANES, LANES), jnp.float32),
            pltpu.VMEM((2, rows, 2 * LANES), jnp.float32),
            pltpu.VMEM((rows, 2 * rows), jnp.bfloat16),
            pltpu.VMEM((1, 4 * rows), jnp.int32),
            pltpu.VMEM((rows, LANES), jnp.int32),
            pltpu.VMEM((2, 1, 2 * rows), jnp.int32),
            pltpu.VMEM((24, LANES), jnp.float32),
            pltpu.VMEM((8, LANES), jnp.float32),
            pltpu.VMEM((n_a, 8, LANES), jnp.float32),
            pltpu.VMEM((n_b, 8, LANES), jnp.float32),
            dma((5, parts)), dma((3,)), dma((KINDS + 4,)), dma((KINDS, parts)),
            *(dma(()),) * 4,
        ],
        compiler_params=pltpu.CompilerParams(
            collective_id=0, has_side_effects=True, vmem_limit_bytes=48 * 1024 * 1024),
        cost_estimate=pl.CostEstimate(
            flops=2 * 32 * rows * rows * width, bytes_accessed=7 * rows * width * 2 + 2 * rows * width * 4,
            transcendentals=24 * rows * rows),
    )(text, image, positive, log_temp, bias)
    scalar = jax.ShapeDtypeStruct((1,), jnp.float32)
    return pl.pallas_call(
        write_out,
        out_shape=(*(jax.ShapeDtypeStruct((rows, width), jnp.float32),) * 2, scalar, scalar, scalar),
        in_specs=[vmem, vmem, vmem],
        out_specs=(hbm, hbm, smem, smem, smem),
        scratch_shapes=[dma((4,))],
        compiler_params=pltpu.CompilerParams(vmem_limit_bytes=1024 * 1024),
    )(*results)


def solution(mesh):
    return jax.shard_map(
        functools.partial(on_device, mesh.shape["dp"]),
        mesh=mesh,
        in_specs=(P("dp", None), P(("dp", "row"), None), P("dp", None), P(), P()),
        out_specs=(P(("dp", "row"), None), P(("dp", "row"), None), P(), P(), P()),
        check_vma=False,
    )
```

```python
import functools

import jax
import jax.numpy as jnp
from jax import lax
from jax.experimental import pallas as pl
from jax.experimental.pallas import tpu as pltpu
from jax.sharding import PartitionSpec as P

MESH = pl.DeviceIdType.MESH
NT = (((1,), (1,)), ((), ()))
LANES = 128

IMG, NEXT, TXT, PREV = range(4)

X_IMG, C_IMG, F_IMG, Z_IMG, F_NEXT, Z_TXT, F_PREV = 0, 1, 2, 3, 5, 7, 9
KINDS = 11
FOR_SIDE = 11
X_NEXT = 14


def kernel(n_dp, text, image, positive, log_temp, bias, grad_text, grad_image, out_sums,
           held, raw, inverses, cosines, slopes, pos, pos_cols, pos_rows, sums, packed, met_a, met_b,
           load_sem, raw_sem, send_sem, recv_sem, send_a, recv_a, send_b, recv_b):
    parts, width = held.shape[2], held.shape[-1]
    rows = parts * LANES
    dp, row = lax.axis_index("dp"), lax.axis_index("row")
    side = row + 1 - 2 * (row % 2)
    opposite = (row + 2) % 4
    quarter = ((row, side), (opposite, (side + 2) % 4))
    up, down = (dp + 1) % n_dp, (dp + n_dp - 1) % n_dp
    first_z, last_z = dp % 4 == 0, dp % 4 == 3
    end_z = jnp.logical_or(first_z, last_z)
    before_last_z = dp % 4 == 2
    core0, core1 = row % 2 == 0, row % 2 == 1
    opposite_side = quarter[1][1]

    n_b = met_b.shape[0]
    n_y = n_dp // n_b
    y, rest = dp // n_b, dp % n_b
    place_a = y * 4 + row
    group_a = [(((y + i // 4) % n_y) * n_b + rest, (row + i % 4) % 4) for i in range(1, 4 * n_y)]
    group_b = [(y * n_b + (rest + i) % n_b, row) for i in range(1, n_b)]

    barrier = pltpu.get_barrier_semaphore()
    greeted = [(near, (row + i) % 4) for near in (up, down) for i in range(4)] + group_a + group_b
    for device in greeted:
        pl.semaphore_signal(barrier, inc=1, device_id=device, device_id_type=MESH)

    def load(source, first, group, pair, k, core):
        first = pl.multiple_of(first + k * LANES, LANES)
        return pltpu.make_async_copy(source.at[pl.ds(first, LANES)], held.at[group, pair, k, core],
                                     load_sem.at[0 if group == IMG else 1 + 2 * pair + core, k])

    def load_image(k):
        return load(image, 0, IMG, 0, k, 0)

    def load_text(pair, core, k):
        return load(text, quarter[pair][core] * rows, TXT, pair, k, core)

    for k in range(parts):
        load_image(k).start()
    pos_copy = pltpu.make_async_copy(positive, pos, raw_sem.at[2])
    for pair, core in ((0, 0), (1, 0), (0, 1), (1, 1)):
        for k in range(parts):
            load_text(pair, core, k).start()
        if core == 0 and pair == 1:
            pos_copy.start()
    own_text = pltpu.make_async_copy(text.at[pl.ds(pl.multiple_of(row * rows, rows), rows)], raw.at[0], raw_sem.at[0])
    own_image = pltpu.make_async_copy(image, raw.at[1], raw_sem.at[1])
    own_text.start()
    own_image.start()

    temp = jnp.exp(jnp.full((8, LANES), log_temp[0], jnp.float32))[0:1, 0:1]
    shift = bias[0]

    def normalise(group, pair, k, core):
        full = held[group, pair, k, core].astype(jnp.float32)
        inverse = lax.rsqrt(jnp.sum(full * full, axis=-1, keepdims=True) + 1e-06)
        held[group, pair, k, core] = (full * inverse).astype(jnp.bfloat16)
        if pair == 0 and core == 0:
            inverses[0 if group == TXT else 1, k] = jnp.broadcast_to(inverse, (LANES, LANES))

    def copy(kind, k, source, target, device, sent=None):
        return pltpu.make_async_remote_copy(
            src_ref=held.at[source], dst_ref=held.at[target],
            send_sem=send_sem.at[kind if sent is None else sent], recv_sem=recv_sem.at[kind, k],
            device_id=device, device_id_type=MESH)

    def x_img(k):
        return copy(X_IMG, k, (IMG, 0, k, 0), (IMG, 1, k, 0), (dp, opposite))

    def x_img_for_side(k):
        return copy(X_IMG, k, (IMG, 0, k, 1), (IMG, 1, k, 0), (dp, opposite_side), FOR_SIDE)

    def c_img(k):
        return copy(C_IMG, k, (IMG, 0, k, 0), (IMG, 0, k, 1), (dp, side))

    def f_img(k):
        return copy(F_IMG, k, (IMG, 1, k, 0), (IMG, 1, k, 1), (dp, side))

    def z_img(pair, k):
        across = jnp.logical_and(first_z, pair == 1)
        return copy(Z_IMG + pair, k, (IMG, jnp.where(across, 0, pair), k, 0), (NEXT, pair, k, 0),
                    (down, jnp.where(across, opposite, row)))

    def x_next(k):
        return copy(Z_IMG + 1, k, (NEXT, 0, k, 0), (NEXT, 1, k, 0), (dp, opposite), X_NEXT)

    def z_img_for_side(pair, k):
        return copy(Z_IMG + pair, k, (IMG, 0, k, 1), (NEXT, pair, k, 0),
                    (down, opposite_side if pair else side), FOR_SIDE + 1 + pair)

    def z_txt(pair, k):
        across = jnp.logical_and(last_z, pair == 1)
        return copy(Z_TXT + pair, k, (TXT, jnp.where(across, 0, pair), k, 0), (PREV, pair, k, 0),
                    (up, jnp.where(across, opposite, row)))

    def z_txt_for_side(pair, k):
        return copy(Z_TXT + pair, k, (TXT, 0, k, 1), (PREV, pair, k, 0),
                    (up, opposite_side if pair else side), FOR_SIDE + 1 + pair)

    def f_next(pair, k):
        return copy(F_NEXT + pair, k, (NEXT, pair, k, 0), (NEXT, pair, k, 1), (dp, side))

    def f_prev(pair, k):
        return copy(F_PREV + pair, k, (PREV, pair, k, 0), (PREV, pair, k, 1), (dp, side))

    sends_x = jnp.logical_or(jnp.logical_not(end_z), core1)
    sends_img = jnp.logical_or(jnp.logical_not(first_z), core0)
    sends_txt = jnp.logical_or(jnp.logical_not(last_z), core0)
    img_for_side = jnp.logical_and(first_z, core0)
    txt_for_side = jnp.logical_and(last_z, core0)
    x_for_side = jnp.logical_and(end_z, core1)

    for k in range(parts):
        load_image(k).wait()
        normalise(IMG, 0, k, 0)
        if k == 0:
            pl.semaphore_wait(barrier, len(greeted))
        c_img(k).start()

        @pl.when(jnp.logical_not(end_z))
        def _():
            x_img(k).start()

        @pl.when(jnp.logical_not(first_z))
        def _():
            z_img(0, k).start()

        if k == 0:
            @pl.when(img_for_side)
            def _():
                z_img(0, k).start()
                z_img(1, k).start()

            @pl.when(x_for_side)
            def _():
                x_img(k).start()

    for k in range(parts):
        load_text(0, 0, k).wait()
        normalise(TXT, 0, k, 0)

        @pl.when(sends_txt)
        def _():
            z_txt(0, k).start()

        load_text(0, 1, k).wait()
        normalise(TXT, 0, k, 1)

        @pl.when(txt_for_side)
        def _():
            z_txt(1, k).start()
            z_txt_for_side(0, k).start()
            z_txt_for_side(1, k).start()

        c_img(k).wait_recv()

        @pl.when(x_for_side)
        def _():
            x_img_for_side(k).start()
            if k + 1 < parts:
                x_img(k + 1).start()

        @pl.when(img_for_side)
        def _():
            z_img_for_side(0, k).start()
            z_img_for_side(1, k).start()
            if k + 1 < parts:
                z_img(0, k + 1).start()
                z_img(1, k + 1).start()

    for k in range(parts):
        load_text(1, 0, k).wait()
        normalise(TXT, 1, k, 0)

        @pl.when(jnp.logical_not(last_z))
        def _():
            z_txt(1, k).start()

    for k in range(parts):
        load_text(1, 1, k).wait()
        normalise(TXT, 1, k, 1)

    pos_copy.wait()
    mine = pos[:, pl.ds(pl.multiple_of(row * rows, LANES), rows)]
    pos_cols[...] = jnp.transpose(jnp.broadcast_to(mine, (LANES, rows)))
    for pair in range(2):
        for k in range(parts):
            for core in range(2):
                at = pl.multiple_of(quarter[pair][core] * rows + k * LANES, LANES)
                pos_rows[pair, :, pl.ds((2 * k + core) * LANES, LANES)] = pos[:, pl.ds(at, LANES)]
    sums[...] = jnp.zeros_like(sums)

    span = 2 * LANES
    step = 64

    def meet(own, group, pieces, total, label, with_sums, fresh=False, between=None):
        mine = held[own, 0, :, 0].reshape(rows, width)
        others = jnp.concatenate([held[group, pair, k].reshape(span, width) for pair, k in pieces], axis=0)
        if len(pieces) <= 2:
            cosines[:, :len(pieces) * span] = lax.dot_general(mine, others, NT, preferred_element_type=jnp.float32)
        for i, (pair, k) in enumerate(pieces):
            here = cosines.at[:, pl.ds((i % 2) * span, span)]
            if len(pieces) > 2 and i % 2 == 0:
                cosines[...] = lax.dot_general(mine, others[i * span:(i + 2) * span], NT, preferred_element_type=jnp.float32)
            for first in range(0, rows, step):
                block = pl.ds(first, step)
                cosine = here[block]
                logits = temp * cosine + shift
                if label is not None:
                    is_pair = label(first, k)
                    logits = jnp.where(is_pair, -logits, logits)
                small = jnp.exp(-jnp.abs(logits))
                upper = 1.0 / (1.0 + small)
                slope = jnp.where(logits >= 0, upper, small * upper)
                if label is not None:
                    slope = jnp.where(is_pair, -slope, slope)
                slopes[block, i * span:(i + 1) * span] = slope.astype(jnp.bfloat16)
                if with_sums:
                    pair_loss = jnp.maximum(logits, 0.0) + jnp.log1p(small)
                    for j, value in enumerate((pair_loss, slope * cosine, slope)):
                        value = jnp.sum(value.reshape(step // 8, 8, span), axis=0)
                        sums[j * 8:(j + 1) * 8] += value[:, :LANES] + value[:, LANES:]
        if between is not None:
            between()
        product = jnp.dot(slopes[:, :len(pieces) * span], others, preferred_element_type=jnp.float32)
        total[...] = product if fresh else total[...] + product

    def text_meets_own(pair, k0, count, fresh=False):
        def label(first, k):
            lane = lax.broadcasted_iota(jnp.int32, (step, LANES), 1) + k * LANES
            at = jnp.concatenate([lane + quarter[pair][core] * rows for core in range(2)], axis=1)
            here = pos_cols[pl.ds(first, step)]
            return jnp.concatenate([here, here], axis=1) == at
        meet(TXT, IMG, [(pair, k0 + i) for i in range(count)], grad_text, label, True, fresh=fresh)

    def image_meets_own(pair, fresh=False):
        def label(first, k):
            at = lax.broadcasted_iota(jnp.int32, (step, span), 0) + (row * rows + first)
            return jnp.broadcast_to(pos_rows[pair, :, pl.ds(k * span, span)], (step, span)) == at
        meet(IMG, TXT, [(pair, k) for k in range(parts)], grad_image, label, False, fresh=fresh)

    image_meets_own(0, True)
    text_meets_own(0, 0, parts, True)
    image_meets_own(1)

    def bytes_of(ref, sent, arrived):
        return pltpu.make_async_remote_copy(src_ref=ref, dst_ref=ref, send_sem=sent, recv_sem=arrived,
                                            device_id=(dp, side), device_id_type=MESH)

    def to_a(i):
        return pltpu.make_async_remote_copy(
            src_ref=packed, dst_ref=met_a.at[place_a], send_sem=send_a, recv_sem=recv_a,
            device_id=group_a[i], device_id_type=MESH)

    def to_b(i):
        return pltpu.make_async_remote_copy(
            src_ref=met_b.at[rest], dst_ref=met_b.at[rest], send_sem=send_b, recv_sem=recv_b,
            device_id=group_b[i], device_id_type=MESH)

    def finish(total, which):
        @pl.loop(0, parts)
        def _(k):
            block = pl.ds(pl.multiple_of(k * LANES, LANES), LANES)
            full = raw[which, block].astype(jnp.float32)
            grad = temp * total[block]
            inverse = inverses[which, k][:, 0:1]
            unit = full * inverse
            along = jnp.sum(unit * grad, axis=-1, keepdims=True)
            total[block] = (grad - unit * along) * inverse

    own_text.wait()
    own_image.wait()
    packed[...] = jnp.zeros_like(packed)

    @pl.loop(0, parts)
    def _(t):
        def pieces(together):
            return [(jnp.where(together, s % 2, s // parts), jnp.where(together, s // 2, s % parts))
                    for s in (2 * t, 2 * t + 1)]

        nexts, prevs = pieces(last_z), pieces(first_z)
        early = t < parts // 2
        x_two = jnp.logical_and(jnp.logical_not(end_z), early)

        @pl.when(x_two)
        def _():
            for i in range(2):
                x_img(2 * t + i).wait_recv()
                f_img(2 * t + i).start()
                z_img(1, 2 * t + i).start()

        def take_nexts():
            for i in range(2):
                z_img(*nexts[i]).wait_recv()
                f_next(*nexts[i]).start()

                @pl.when(jnp.logical_and(before_last_z, early))
                def _():
                    x_next(nexts[i][1]).start()

        def take_prevs():
            for i in range(2):
                z_txt(*prevs[i]).wait_recv()
                f_prev(*prevs[i]).start()

        def meet_prevs():
            for i in range(2):
                f_prev(*prevs[i]).wait_recv()
            meet(IMG, PREV, prevs, grad_image, None, False)

        pl.when(jnp.logical_not(last_z))(take_nexts)
        pl.when(jnp.logical_not(first_z))(take_prevs)

        @pl.when(end_z)
        def _():
            x_img(t).wait_recv()
            f_img(t).start()

        pl.when(last_z)(meet_prevs)

        @pl.when(x_two)
        def _():
            for i in range(2):
                f_img(2 * t + i).wait_recv()
            text_meets_own(1, 2 * t, 2)

        @pl.when(end_z)
        def _():
            f_img(t).wait_recv()
            text_meets_own(1, t, 1)

        last = t == parts - 1

        def start_sums():
            @pl.when(last)
            def _():
                for i in range(3):
                    packed[i:i + 1] = jnp.sum(sums[8 * i:8 * (i + 1)], axis=0, keepdims=True)
                for i in range(len(group_a)):
                    to_a(i).start()

        pl.when(last_z)(take_nexts)
        for i in range(2):
            f_next(*nexts[i]).wait_recv()
        meet(TXT, NEXT, nexts, grad_text, None, True, between=start_sums)
        pl.when(first_z)(take_prevs)

        @pl.when(last)
        def _():
            finish(grad_text, 0)
            met_a[place_a] = packed[...]
            bytes_of(met_a.at[pl.ds(0, len(group_a))], send_a, recv_a).wait_recv()
            met_b[rest] = functools.reduce(lambda a, b: a + b, [met_a[i] for i in range(4 * n_y)])
            for i in range(len(group_b)):
                to_b(i).start()

        pl.when(jnp.logical_not(last_z))(meet_prevs)

    finish(grad_image, 1)
    bytes_of(met_b.at[pl.ds(0, len(group_b))], send_b, recv_b).wait_recv()
    total = functools.reduce(lambda a, b: a + b, [met_b[i] for i in range(n_b)])
    count = rows * 4 * n_dp
    out_sums[...] = total / count
    out_sums[1:2] = temp * total[1:2] / count

    def all_sent(*kinds):
        for kind in kinds:
            bytes_of(raw.at[0], send_sem.at[kind], recv_sem.at[0, 0]).wait_send()

    all_sent(C_IMG, F_IMG, F_NEXT, F_NEXT + 1, F_PREV, F_PREV + 1)
    for sends, kinds in ((sends_x, (X_IMG,)), (x_for_side, (FOR_SIDE,)), (before_last_z, (X_NEXT,)),
                         (sends_img, (Z_IMG,)), (jnp.logical_and(sends_img, jnp.logical_not(last_z)), (Z_IMG + 1,)),
                         (img_for_side, (FOR_SIDE + 1, FOR_SIDE + 2)),
                         (sends_txt, (Z_TXT, Z_TXT + 1)), (txt_for_side, (FOR_SIDE + 1, FOR_SIDE + 2))):
        @pl.when(sends)
        def _():
            all_sent(*kinds)

    bytes_of(met_a.at[pl.ds(0, len(group_a))], send_a, recv_a).wait_send()
    bytes_of(met_b.at[pl.ds(0, len(group_b))], send_b, recv_b).wait_send()


def write_out(grad_text, grad_image, sums, out_text, out_image, loss, grad_log_temp, grad_bias, sem):
    half = grad_text.shape[0] // 2
    copies = [pltpu.make_async_copy(source.at[pl.ds(i * half, half)], target.at[pl.ds(i * half, half)], sem.at[2 * j + i])
              for j, (source, target) in enumerate(((grad_text, out_text), (grad_image, out_image))) for i in range(2)]
    for copy in copies:
        copy.start()
    for j, out in enumerate((loss, grad_log_temp, grad_bias)):
        out[0] = jnp.sum(sums[j:j + 1])
    for copy in copies:
        copy.wait()


def on_device(n_dp, text, image, positive, log_temp, bias):
    rows, width = image.shape
    parts = rows // LANES
    n_b = min(n_dp, 8)
    n_a = 4 * (n_dp // n_b)
    vmem, smem, hbm = (pl.BlockSpec(memory_space=m) for m in (pltpu.VMEM, pltpu.SMEM, pltpu.HBM))
    dma = pltpu.SemaphoreType.DMA
    results = pl.pallas_call(
        functools.partial(kernel, n_dp),
        out_shape=(
            jax.ShapeDtypeStruct((rows, width), jnp.float32),
            jax.ShapeDtypeStruct((rows, width), jnp.float32),
            jax.ShapeDtypeStruct((8, LANES), jnp.float32),
        ),
        in_specs=[hbm, hbm, hbm, smem, smem],
        out_specs=(vmem, vmem, vmem),
        scratch_shapes=[
            pltpu.VMEM((4, 2, parts, 2, LANES, width), jnp.bfloat16),
            pltpu.VMEM((2, rows, width), jnp.bfloat16),
            pltpu.VMEM((2, parts, LANES, LANES), jnp.float32),
            pltpu.VMEM((rows, 4 * LANES), jnp.float32),
            pltpu.VMEM((rows, 2 * rows), jnp.bfloat16),
            pltpu.VMEM((1, 4 * rows), jnp.int32),
            pltpu.VMEM((rows, LANES), jnp.int32),
            pltpu.VMEM((2, 1, 2 * rows), jnp.int32),
            pltpu.VMEM((24, LANES), jnp.float32),
            pltpu.VMEM((8, LANES), jnp.float32),
            pltpu.VMEM((n_a, 8, LANES), jnp.float32),
            pltpu.VMEM((n_b, 8, LANES), jnp.float32),
            dma((5, parts)), dma((3,)), dma((KINDS + 4,)), dma((KINDS, parts)),
            *(dma(()),) * 4,
        ],
        compiler_params=pltpu.CompilerParams(
            collective_id=0, has_side_effects=True, vmem_limit_bytes=48 * 1024 * 1024),
        cost_estimate=pl.CostEstimate(
            flops=2 * 32 * rows * rows * width, bytes_accessed=7 * rows * width * 2 + 2 * rows * width * 4,
            transcendentals=24 * rows * rows),
    )(text, image, positive, log_temp, bias)
    scalar = jax.ShapeDtypeStruct((1,), jnp.float32)
    return pl.pallas_call(
        write_out,
        out_shape=(*(jax.ShapeDtypeStruct((rows, width), jnp.float32),) * 2, scalar, scalar, scalar),
        in_specs=[vmem, vmem, vmem],
        out_specs=(hbm, hbm, smem, smem, smem),
        scratch_shapes=[dma((4,))],
        compiler_params=pltpu.CompilerParams(vmem_limit_bytes=1024 * 1024),
    )(*results)


def solution(mesh):
    return jax.shard_map(
        functools.partial(on_device, mesh.shape["dp"]),
        mesh=mesh,
        in_specs=(P("dp", None), P(("dp", "row"), None), P("dp", None), P(), P()),
        out_specs=(P(("dp", "row"), None), P(("dp", "row"), None), P(), P(), P()),
        check_vma=False,
    )
```

```python
import functools

import jax
import jax.numpy as jnp
from jax import lax
from jax.experimental import pallas as pl
from jax.experimental.pallas import tpu as pltpu
from jax.sharding import PartitionSpec as P

MESH = pl.DeviceIdType.MESH
NT = (((1,), (1,)), ((), ()))
LANES = 128

IMG, NEXT, TXT, PREV = range(4)

X_IMG, C_IMG, F_IMG, Z_IMG, F_NEXT, Z_TXT, F_PREV = 0, 1, 2, 3, 5, 7, 9
KINDS = 11
FOR_SIDE = 11
X_NEXT = 14


def kernel(n_dp, text, image, positive, log_temp, bias, grad_text, grad_image, out_sums,
           held, raw, inverses, cosines, slopes, pos, pos_cols, pos_rows, sums, packed, met_a, met_b,
           load_sem, raw_sem, send_sem, recv_sem, send_a, recv_a, send_b, recv_b):
    parts, width = held.shape[2], held.shape[-1]
    rows = parts * LANES
    dp, row = lax.axis_index("dp"), lax.axis_index("row")
    side = row + 1 - 2 * (row % 2)
    opposite = (row + 2) % 4
    quarter = ((row, side), (opposite, (side + 2) % 4))
    up, down = (dp + 1) % n_dp, (dp + n_dp - 1) % n_dp
    first_z, last_z = dp % 4 == 0, dp % 4 == 3
    end_z = jnp.logical_or(first_z, last_z)
    before_last_z = dp % 4 == 2
    core0, core1 = row % 2 == 0, row % 2 == 1
    opposite_side = quarter[1][1]

    n_b = met_b.shape[0]
    n_y = n_dp // n_b
    y, rest = dp // n_b, dp % n_b
    place_a = y * 4 + row
    group_a = [(((y + i // 4) % n_y) * n_b + rest, (row + i % 4) % 4) for i in range(1, 4 * n_y)]
    group_b = [(y * n_b + (rest + i) % n_b, row) for i in range(1, n_b)]

    barrier = pltpu.get_barrier_semaphore()
    greeted = [(near, (row + i) % 4) for near in (up, down) for i in range(4)] + group_a + group_b
    for device in greeted:
        pl.semaphore_signal(barrier, inc=1, device_id=device, device_id_type=MESH)

    def load(source, first, group, pair, k, core):
        first = pl.multiple_of(first + k * LANES, LANES)
        return pltpu.make_async_copy(source.at[pl.ds(first, LANES)], held.at[group, pair, k, core],
                                     load_sem.at[2 * pair + core, k])

    def load_text(pair, core, k):
        return load(text, quarter[pair][core] * rows, TXT, pair, k, core)

    pos_copy = pltpu.make_async_copy(positive, pos, raw_sem.at[1])
    for pair, core in ((0, 0), (1, 0), (0, 1), (1, 1)):
        for k in range(parts):
            load_text(pair, core, k).start()
        if core == 0 and pair == 1:
            pos_copy.start()
    own_text = pltpu.make_async_copy(text.at[pl.ds(pl.multiple_of(row * rows, rows), rows)], raw, raw_sem.at[0])
    own_text.start()

    temp = jnp.exp(jnp.full((8, LANES), log_temp[0], jnp.float32))[0:1, 0:1]
    shift = bias[0]

    def normalise(group, pair, k, core):
        source = image[k * LANES:(k + 1) * LANES] if group == IMG else held[group, pair, k, core]
        full = source.astype(jnp.float32)
        inverse = lax.rsqrt(jnp.sum(full * full, axis=-1, keepdims=True) + 1e-06)
        held[group, pair, k, core] = (full * inverse).astype(jnp.bfloat16)
        if pair == 0 and core == 0:
            inverses[0 if group == TXT else 1, k] = jnp.broadcast_to(inverse, (LANES, LANES))

    def copy(kind, k, source, target, device, sent=None):
        return pltpu.make_async_remote_copy(
            src_ref=held.at[source], dst_ref=held.at[target],
            send_sem=send_sem.at[kind if sent is None else sent], recv_sem=recv_sem.at[kind, k],
            device_id=device, device_id_type=MESH)

    def x_img(k):
        return copy(X_IMG, k, (IMG, 0, k, 0), (IMG, 1, k, 0), (dp, opposite))

    def x_img_for_side(k):
        return copy(X_IMG, k, (IMG, 0, k, 1), (IMG, 1, k, 0), (dp, opposite_side), FOR_SIDE)

    def c_img(k):
        return copy(C_IMG, k, (IMG, 0, k, 0), (IMG, 0, k, 1), (dp, side))

    def f_img(k):
        return copy(F_IMG, k, (IMG, 1, k, 0), (IMG, 1, k, 1), (dp, side))

    def z_img(pair, k):
        across = jnp.logical_and(first_z, pair == 1)
        return copy(Z_IMG + pair, k, (IMG, jnp.where(across, 0, pair), k, 0), (NEXT, pair, k, 0),
                    (down, jnp.where(across, opposite, row)))

    def x_next(k):
        return copy(Z_IMG + 1, k, (NEXT, 0, k, 0), (NEXT, 1, k, 0), (dp, opposite), X_NEXT)

    def z_img_for_side(pair, k):
        return copy(Z_IMG + pair, k, (IMG, 0, k, 1), (NEXT, pair, k, 0),
                    (down, opposite_side if pair else side), FOR_SIDE + 1 + pair)

    def z_txt(pair, k):
        across = jnp.logical_and(last_z, pair == 1)
        return copy(Z_TXT + pair, k, (TXT, jnp.where(across, 0, pair), k, 0), (PREV, pair, k, 0),
                    (up, jnp.where(across, opposite, row)))

    def z_txt_for_side(pair, k):
        return copy(Z_TXT + pair, k, (TXT, 0, k, 1), (PREV, pair, k, 0),
                    (up, opposite_side if pair else side), FOR_SIDE + 1 + pair)

    def f_next(pair, k):
        return copy(F_NEXT + pair, k, (NEXT, pair, k, 0), (NEXT, pair, k, 1), (dp, side))

    def f_prev(pair, k):
        return copy(F_PREV + pair, k, (PREV, pair, k, 0), (PREV, pair, k, 1), (dp, side))

    sends_x = jnp.logical_or(jnp.logical_not(end_z), core1)
    sends_img = jnp.logical_or(jnp.logical_not(first_z), core0)
    sends_txt = jnp.logical_or(jnp.logical_not(last_z), core0)
    img_for_side = jnp.logical_and(first_z, core0)
    txt_for_side = jnp.logical_and(last_z, core0)
    x_for_side = jnp.logical_and(end_z, core1)

    for k in range(parts):
        normalise(IMG, 0, k, 0)
        if k == 0:
            pl.semaphore_wait(barrier, len(greeted))
        c_img(k).start()

        @pl.when(jnp.logical_not(end_z))
        def _():
            x_img(k).start()

        @pl.when(jnp.logical_not(first_z))
        def _():
            z_img(0, k).start()

        if k == 0:
            @pl.when(img_for_side)
            def _():
                z_img(0, k).start()
                z_img(1, k).start()

            @pl.when(x_for_side)
            def _():
                x_img(k).start()

    for k in range(parts):
        load_text(0, 0, k).wait()
        normalise(TXT, 0, k, 0)

        @pl.when(sends_txt)
        def _():
            z_txt(0, k).start()

        load_text(0, 1, k).wait()
        normalise(TXT, 0, k, 1)

        @pl.when(txt_for_side)
        def _():
            z_txt(1, k).start()
            z_txt_for_side(0, k).start()
            z_txt_for_side(1, k).start()

        c_img(k).wait_recv()

        @pl.when(x_for_side)
        def _():
            x_img_for_side(k).start()
            if k + 1 < parts:
                x_img(k + 1).start()

        @pl.when(img_for_side)
        def _():
            z_img_for_side(0, k).start()
            z_img_for_side(1, k).start()
            if k + 1 < parts:
                z_img(0, k + 1).start()
                z_img(1, k + 1).start()

    for k in range(parts):
        load_text(1, 0, k).wait()
        normalise(TXT, 1, k, 0)

        @pl.when(jnp.logical_not(last_z))
        def _():
            z_txt(1, k).start()

    for k in range(parts):
        load_text(1, 1, k).wait()
        normalise(TXT, 1, k, 1)

    pos_copy.wait()
    mine = pos[:, pl.ds(pl.multiple_of(row * rows, LANES), rows)]
    pos_cols[...] = jnp.transpose(jnp.broadcast_to(mine, (LANES, rows)))
    for pair in range(2):
        for k in range(parts):
            for core in range(2):
                at = pl.multiple_of(quarter[pair][core] * rows + k * LANES, LANES)
                pos_rows[pair, :, pl.ds((2 * k + core) * LANES, LANES)] = pos[:, pl.ds(at, LANES)]
    sums[...] = jnp.zeros_like(sums)

    span = 2 * LANES
    step = 64

    def meet(own, group, pieces, total, label, with_sums, fresh=False, between=None):
        mine = held[own, 0, :, 0].reshape(rows, width)
        others = jnp.concatenate([held[group, pair, k].reshape(span, width) for pair, k in pieces], axis=0)
        if len(pieces) <= 2:
            cosines[:, :len(pieces) * span] = lax.dot_general(mine, others, NT, preferred_element_type=jnp.float32)
        for i, (pair, k) in enumerate(pieces):
            here = cosines.at[:, pl.ds((i % 2) * span, span)]
            if len(pieces) > 2 and i % 2 == 0:
                cosines[...] = lax.dot_general(mine, others[i * span:(i + 2) * span], NT, preferred_element_type=jnp.float32)
            for first in range(0, rows, step):
                block = pl.ds(first, step)
                cosine = here[block]
                logits = temp * cosine + shift
                if label is not None:
                    is_pair = label(first, k)
                    logits = jnp.where(is_pair, -logits, logits)
                small = jnp.exp(-jnp.abs(logits))
                upper = 1.0 / (1.0 + small)
                slope = jnp.where(logits >= 0, upper, small * upper)
                if label is not None:
                    slope = jnp.where(is_pair, -slope, slope)
                slopes[block, i * span:(i + 1) * span] = slope.astype(jnp.bfloat16)
                if with_sums:
                    pair_loss = jnp.maximum(logits, 0.0) + jnp.log1p(small)
                    for j, value in enumerate((pair_loss, slope * cosine, slope)):
                        value = jnp.sum(value.reshape(step // 8, 8, span), axis=0)
                        sums[j * 8:(j + 1) * 8] += value[:, :LANES] + value[:, LANES:]
        if between is not None:
            between()
        product = jnp.dot(slopes[:, :len(pieces) * span], others, preferred_element_type=jnp.float32)
        total[...] = product if fresh else total[...] + product

    def text_meets_own(pair, k0, count, fresh=False):
        def label(first, k):
            lane = lax.broadcasted_iota(jnp.int32, (step, LANES), 1) + k * LANES
            at = jnp.concatenate([lane + quarter[pair][core] * rows for core in range(2)], axis=1)
            here = pos_cols[pl.ds(first, step)]
            return jnp.concatenate([here, here], axis=1) == at
        meet(TXT, IMG, [(pair, k0 + i) for i in range(count)], grad_text, label, True, fresh=fresh)

    def image_meets_own(pair, fresh=False):
        def label(first, k):
            at = lax.broadcasted_iota(jnp.int32, (step, span), 0) + (row * rows + first)
            return jnp.broadcast_to(pos_rows[pair, :, pl.ds(k * span, span)], (step, span)) == at
        meet(IMG, TXT, [(pair, k) for k in range(parts)], grad_image, label, False, fresh=fresh)

    image_meets_own(0, True)
    text_meets_own(0, 0, parts, True)
    image_meets_own(1)

    def bytes_of(ref, sent, arrived):
        return pltpu.make_async_remote_copy(src_ref=ref, dst_ref=ref, send_sem=sent, recv_sem=arrived,
                                            device_id=(dp, side), device_id_type=MESH)

    def to_a(i):
        return pltpu.make_async_remote_copy(
            src_ref=packed, dst_ref=met_a.at[place_a], send_sem=send_a, recv_sem=recv_a,
            device_id=group_a[i], device_id_type=MESH)

    def to_b(i):
        return pltpu.make_async_remote_copy(
            src_ref=met_b.at[rest], dst_ref=met_b.at[rest], send_sem=send_b, recv_sem=recv_b,
            device_id=group_b[i], device_id_type=MESH)

    def finish(total, which):
        @pl.loop(0, parts)
        def _(k):
            block = pl.ds(pl.multiple_of(k * LANES, LANES), LANES)
            full = (raw, image)[which][block].astype(jnp.float32)
            grad = temp * total[block]
            inverse = inverses[which, k][:, 0:1]
            unit = full * inverse
            along = jnp.sum(unit * grad, axis=-1, keepdims=True)
            total[block] = (grad - unit * along) * inverse

    own_text.wait()
    packed[...] = jnp.zeros_like(packed)

    @pl.loop(0, parts)
    def _(t):
        def pieces(together):
            return [(jnp.where(together, s % 2, s // parts), jnp.where(together, s // 2, s % parts))
                    for s in (2 * t, 2 * t + 1)]

        nexts, prevs = pieces(last_z), pieces(first_z)
        early = t < parts // 2
        x_two = jnp.logical_and(jnp.logical_not(end_z), early)

        @pl.when(x_two)
        def _():
            for i in range(2):
                x_img(2 * t + i).wait_recv()
                f_img(2 * t + i).start()
                z_img(1, 2 * t + i).start()

        def take_nexts():
            for i in range(2):
                z_img(*nexts[i]).wait_recv()
                f_next(*nexts[i]).start()

                @pl.when(jnp.logical_and(before_last_z, early))
                def _():
                    x_next(nexts[i][1]).start()

        def take_prevs():
            for i in range(2):
                z_txt(*prevs[i]).wait_recv()
                f_prev(*prevs[i]).start()

        def meet_prevs():
            for i in range(2):
                f_prev(*prevs[i]).wait_recv()
            meet(IMG, PREV, prevs, grad_image, None, False)

        last = t == parts - 1

        def start_sums():
            @pl.when(last)
            def _():
                for i in range(3):
                    packed[i:i + 1] = jnp.sum(sums[8 * i:8 * (i + 1)], axis=0, keepdims=True)
                for i in range(len(group_a)):
                    to_a(i).start()

        def meet_nexts(between=None):
            for i in range(2):
                f_next(*nexts[i]).wait_recv()
            meet(TXT, NEXT, nexts, grad_text, None, True, between=between)

        pl.when(jnp.logical_not(last_z))(take_nexts)
        pl.when(jnp.logical_not(first_z))(take_prevs)
        pl.when(last_z)(meet_prevs)
        pl.when(jnp.logical_not(last_z))(meet_nexts)

        @pl.when(x_two)
        def _():
            for i in range(2):
                f_img(2 * t + i).wait_recv()
            text_meets_own(1, 2 * t, 2)

        @pl.when(end_z)
        def _():
            x_img(t).wait_recv()
            f_img(t).start()

        pl.when(first_z)(take_prevs)
        pl.when(last_z)(take_nexts)

        @pl.when(end_z)
        def _():
            f_img(t).wait_recv()
            text_meets_own(1, t, 1)

        pl.when(last_z)(functools.partial(meet_nexts, start_sums))
        pl.when(jnp.logical_not(last_z))(start_sums)

        @pl.when(last)
        def _():
            finish(grad_text, 0)
            met_a[place_a] = packed[...]
            bytes_of(met_a.at[pl.ds(0, len(group_a))], send_a, recv_a).wait_recv()
            met_b[rest] = functools.reduce(lambda a, b: a + b, [met_a[i] for i in range(4 * n_y)])
            for i in range(len(group_b)):
                to_b(i).start()

        pl.when(jnp.logical_not(last_z))(meet_prevs)

    finish(grad_image, 1)
    bytes_of(met_b.at[pl.ds(0, len(group_b))], send_b, recv_b).wait_recv()
    total = functools.reduce(lambda a, b: a + b, [met_b[i] for i in range(n_b)])
    count = rows * 4 * n_dp
    out_sums[...] = total / count
    out_sums[1:2] = temp * total[1:2] / count

    def all_sent(*kinds):
        for kind in kinds:
            bytes_of(raw, send_sem.at[kind], recv_sem.at[0, 0]).wait_send()

    all_sent(C_IMG, F_IMG, F_NEXT, F_NEXT + 1, F_PREV, F_PREV + 1)
    for sends, kinds in ((sends_x, (X_IMG,)), (x_for_side, (FOR_SIDE,)), (before_last_z, (X_NEXT,)),
                         (sends_img, (Z_IMG,)), (jnp.logical_and(sends_img, jnp.logical_not(last_z)), (Z_IMG + 1,)),
                         (img_for_side, (FOR_SIDE + 1, FOR_SIDE + 2)),
                         (sends_txt, (Z_TXT, Z_TXT + 1)), (txt_for_side, (FOR_SIDE + 1, FOR_SIDE + 2))):
        @pl.when(sends)
        def _():
            all_sent(*kinds)

    bytes_of(met_a.at[pl.ds(0, len(group_a))], send_a, recv_a).wait_send()
    bytes_of(met_b.at[pl.ds(0, len(group_b))], send_b, recv_b).wait_send()


def write_out(grad_text, grad_image, sums, out_text, out_image, loss, grad_log_temp, grad_bias, sem):
    part = grad_text.shape[0] // 4
    copies = [pltpu.make_async_copy(source.at[pl.ds(i * part, part)], target.at[pl.ds(i * part, part)], sem.at[4 * j + i])
              for j, (source, target) in enumerate(((grad_text, out_text), (grad_image, out_image))) for i in range(4)]
    for copy in copies:
        copy.start()
    for j, out in enumerate((loss, grad_log_temp, grad_bias)):
        out[0] = jnp.sum(sums[j:j + 1])
    for copy in copies:
        copy.wait()


def on_device(n_dp, text, image, positive, log_temp, bias):
    rows, width = image.shape
    parts = rows // LANES
    n_b = min(n_dp, 8)
    n_a = 4 * (n_dp // n_b)
    vmem, smem, hbm = (pl.BlockSpec(memory_space=m) for m in (pltpu.VMEM, pltpu.SMEM, pltpu.HBM))
    dma = pltpu.SemaphoreType.DMA
    results = pl.pallas_call(
        functools.partial(kernel, n_dp),
        out_shape=(
            jax.ShapeDtypeStruct((rows, width), jnp.float32),
            jax.ShapeDtypeStruct((rows, width), jnp.float32),
            jax.ShapeDtypeStruct((8, LANES), jnp.float32),
        ),
        in_specs=[hbm, vmem, hbm, smem, smem],
        out_specs=(vmem, vmem, vmem),
        scratch_shapes=[
            pltpu.VMEM((4, 2, parts, 2, LANES, width), jnp.bfloat16),
            pltpu.VMEM((rows, width), jnp.bfloat16),
            pltpu.VMEM((2, parts, LANES, LANES), jnp.float32),
            pltpu.VMEM((rows, 4 * LANES), jnp.float32),
            pltpu.VMEM((rows, 2 * rows), jnp.bfloat16),
            pltpu.VMEM((1, 4 * rows), jnp.int32),
            pltpu.VMEM((rows, LANES), jnp.int32),
            pltpu.VMEM((2, 1, 2 * rows), jnp.int32),
            pltpu.VMEM((24, LANES), jnp.float32),
            pltpu.VMEM((8, LANES), jnp.float32),
            pltpu.VMEM((n_a, 8, LANES), jnp.float32),
            pltpu.VMEM((n_b, 8, LANES), jnp.float32),
            dma((4, parts)), dma((2,)), dma((KINDS + 4,)), dma((KINDS, parts)),
            *(dma(()),) * 4,
        ],
        compiler_params=pltpu.CompilerParams(
            collective_id=0, has_side_effects=True, vmem_limit_bytes=48 * 1024 * 1024),
        cost_estimate=pl.CostEstimate(
            flops=2 * 32 * rows * rows * width, bytes_accessed=7 * rows * width * 2 + 2 * rows * width * 4,
            transcendentals=24 * rows * rows),
    )(text, image, positive, log_temp, bias)
    scalar = jax.ShapeDtypeStruct((1,), jnp.float32)
    return pl.pallas_call(
        write_out,
        out_shape=(*(jax.ShapeDtypeStruct((rows, width), jnp.float32),) * 2, scalar, scalar, scalar),
        in_specs=[vmem, vmem, vmem],
        out_specs=(hbm, hbm, smem, smem, smem),
        scratch_shapes=[dma((8,))],
        compiler_params=pltpu.CompilerParams(vmem_limit_bytes=1024 * 1024),
    )(*results)


def solution(mesh):
    return jax.shard_map(
        functools.partial(on_device, mesh.shape["dp"]),
        mesh=mesh,
        in_specs=(P("dp", None), P(("dp", "row"), None), P("dp", None), P(), P()),
        out_specs=(P(("dp", "row"), None), P(("dp", "row"), None), P(), P(), P()),
        check_vma=False,
    )
```

```python
import functools

import jax
import jax.numpy as jnp
from jax import lax
from jax.experimental import pallas as pl
from jax.experimental.pallas import tpu as pltpu
from jax.sharding import PartitionSpec as P

MESH = pl.DeviceIdType.MESH
NT = (((1,), (1,)), ((), ()))
LANES = 128

IMG, NEXT, TXT, PREV = range(4)

X_IMG, C_IMG, F_IMG, Z_IMG, F_NEXT, Z_TXT, F_PREV = 0, 1, 2, 3, 5, 7, 9
KINDS = 11
FOR_SIDE = 11
X_NEXT = 14


def kernel(n_dp, text, image, positive, log_temp, bias, grad_text, grad_image, out_sums,
           held, raw, inverses, cosines, slopes, pos, pos_cols, pos_rows, sums, packed, met_a, met_b,
           load_sem, raw_sem, send_sem, recv_sem, send_a, recv_a, send_b, recv_b):
    parts, width = held.shape[2], held.shape[-1]
    rows = parts * LANES
    dp, row = lax.axis_index("dp"), lax.axis_index("row")
    side = row + 1 - 2 * (row % 2)
    opposite = (row + 2) % 4
    quarter = ((row, side), (opposite, (side + 2) % 4))
    up, down = (dp + 1) % n_dp, (dp + n_dp - 1) % n_dp
    first_z, last_z = dp % 4 == 0, dp % 4 == 3
    end_z = jnp.logical_or(first_z, last_z)
    before_last_z = dp % 4 == 2
    core0, core1 = row % 2 == 0, row % 2 == 1
    opposite_side = quarter[1][1]

    n_b = met_b.shape[0]
    n_y = n_dp // n_b
    y, rest = dp // n_b, dp % n_b
    place_a = y * 4 + row
    group_a = [(((y + i // 4) % n_y) * n_b + rest, (row + i % 4) % 4) for i in range(1, 4 * n_y)]
    group_b = [(y * n_b + (rest + i) % n_b, row) for i in range(1, n_b)]

    barrier = pltpu.get_barrier_semaphore()
    greeted = [(near, (row + i) % 4) for near in (up, down) for i in range(4)] + group_a + group_b
    for device in greeted:
        pl.semaphore_signal(barrier, inc=1, device_id=device, device_id_type=MESH)

    def load(source, first, group, pair, k, core):
        first = pl.multiple_of(first + k * LANES, LANES)
        return pltpu.make_async_copy(source.at[pl.ds(first, LANES)], held.at[group, pair, k, core],
                                     load_sem.at[2 * pair + core, k])

    def load_text(pair, core, k):
        return load(text, quarter[pair][core] * rows, TXT, pair, k, core)

    pos_copy = pltpu.make_async_copy(positive, pos, raw_sem.at[1])
    for pair, core in ((0, 0), (1, 0), (0, 1), (1, 1)):
        for k in range(parts):
            load_text(pair, core, k).start()
        if core == 0 and pair == 1:
            pos_copy.start()
    own_text = pltpu.make_async_copy(text.at[pl.ds(pl.multiple_of(row * rows, rows), rows)], raw, raw_sem.at[0])
    own_text.start()

    temp = jnp.exp(jnp.full((8, LANES), log_temp[0], jnp.float32))[0:1, 0:1]
    shift = bias[0]

    def normalise(group, pair, k, core):
        source = image[k * LANES:(k + 1) * LANES] if group == IMG else held[group, pair, k, core]
        full = source.astype(jnp.float32)
        inverse = lax.rsqrt(jnp.sum(full * full, axis=-1, keepdims=True) + 1e-06)
        held[group, pair, k, core] = (full * inverse).astype(jnp.bfloat16)
        if pair == 0 and core == 0:
            inverses[0 if group == TXT else 1, k] = jnp.broadcast_to(inverse, (LANES, LANES))

    def copy(kind, k, source, target, device, sent=None):
        return pltpu.make_async_remote_copy(
            src_ref=held.at[source], dst_ref=held.at[target],
            send_sem=send_sem.at[kind if sent is None else sent], recv_sem=recv_sem.at[kind, k],
            device_id=device, device_id_type=MESH)

    def x_img(k):
        return copy(X_IMG, k, (IMG, 0, k, 0), (IMG, 1, k, 0), (dp, opposite))

    def x_img_for_side(k):
        return copy(X_IMG, k, (IMG, 0, k, 1), (IMG, 1, k, 0), (dp, opposite_side), FOR_SIDE)

    def c_img(k):
        return copy(C_IMG, k, (IMG, 0, k, 0), (IMG, 0, k, 1), (dp, side))

    def f_img(k):
        return copy(F_IMG, k, (IMG, 1, k, 0), (IMG, 1, k, 1), (dp, side))

    def z_img(pair, k):
        across = jnp.logical_and(first_z, pair == 1)
        return copy(Z_IMG + pair, k, (IMG, jnp.where(across, 0, pair), k, 0), (NEXT, pair, k, 0),
                    (down, jnp.where(across, opposite, row)))

    def x_next(k):
        return copy(Z_IMG + 1, k, (NEXT, 0, k, 0), (NEXT, 1, k, 0), (dp, opposite), X_NEXT)

    def z_img_for_side(pair, k):
        return copy(Z_IMG + pair, k, (IMG, 0, k, 1), (NEXT, pair, k, 0),
                    (down, opposite_side if pair else side), FOR_SIDE + 1 + pair)

    def z_txt(pair, k):
        across = jnp.logical_and(last_z, pair == 1)
        return copy(Z_TXT + pair, k, (TXT, jnp.where(across, 0, pair), k, 0), (PREV, pair, k, 0),
                    (up, jnp.where(across, opposite, row)))

    def z_txt_for_side(pair, k):
        return copy(Z_TXT + pair, k, (TXT, 0, k, 1), (PREV, pair, k, 0),
                    (up, opposite_side if pair else side), FOR_SIDE + 1 + pair)

    def f_next(pair, k):
        return copy(F_NEXT + pair, k, (NEXT, pair, k, 0), (NEXT, pair, k, 1), (dp, side))

    def f_prev(pair, k):
        return copy(F_PREV + pair, k, (PREV, pair, k, 0), (PREV, pair, k, 1), (dp, side))

    sends_x = jnp.logical_or(jnp.logical_not(end_z), core1)
    sends_img = jnp.logical_or(jnp.logical_not(first_z), core0)
    sends_txt = jnp.logical_or(jnp.logical_not(last_z), core0)
    img_for_side = jnp.logical_and(first_z, core0)
    txt_for_side = jnp.logical_and(last_z, core0)
    x_for_side = jnp.logical_and(end_z, core1)

    def send_texts(k):
        load_text(0, 0, k).wait()
        normalise(TXT, 0, k, 0)

        @pl.when(sends_txt)
        def _():
            z_txt(0, k).start()

        load_text(0, 1, k).wait()
        normalise(TXT, 0, k, 1)

        @pl.when(txt_for_side)
        def _():
            z_txt(1, k).start()
            z_txt_for_side(0, k).start()
            z_txt_for_side(1, k).start()

    for k in range(parts):
        normalise(IMG, 0, k, 0)
        if k == 0:
            pl.semaphore_wait(barrier, len(greeted))
            pl.when(last_z)(functools.partial(send_texts, 0))
        c_img(k).start()

        @pl.when(jnp.logical_not(end_z))
        def _():
            x_img(k).start()

        @pl.when(jnp.logical_not(first_z))
        def _():
            z_img(0, k).start()

        if k == 0:
            @pl.when(img_for_side)
            def _():
                z_img(0, k).start()
                z_img(1, k).start()

            @pl.when(x_for_side)
            def _():
                x_img(k).start()

    for k in range(parts):
        if k == 0:
            pl.when(jnp.logical_not(last_z))(functools.partial(send_texts, 0))
        else:
            send_texts(k)

        c_img(k).wait_recv()

        @pl.when(x_for_side)
        def _():
            x_img_for_side(k).start()
            if k + 1 < parts:
                x_img(k + 1).start()

        @pl.when(img_for_side)
        def _():
            z_img_for_side(0, k).start()
            z_img_for_side(1, k).start()
            if k + 1 < parts:
                z_img(0, k + 1).start()
                z_img(1, k + 1).start()

    for k in range(parts):
        load_text(1, 0, k).wait()
        normalise(TXT, 1, k, 0)

        @pl.when(jnp.logical_not(last_z))
        def _():
            z_txt(1, k).start()

    for k in range(parts):
        load_text(1, 1, k).wait()
        normalise(TXT, 1, k, 1)

    pos_copy.wait()
    mine = pos[:, pl.ds(pl.multiple_of(row * rows, LANES), rows)]
    pos_cols[...] = jnp.transpose(jnp.broadcast_to(mine, (LANES, rows)))
    for pair in range(2):
        for k in range(parts):
            for core in range(2):
                at = pl.multiple_of(quarter[pair][core] * rows + k * LANES, LANES)
                pos_rows[pair, :, pl.ds((2 * k + core) * LANES, LANES)] = pos[:, pl.ds(at, LANES)]
    sums[...] = jnp.zeros_like(sums)

    span = 2 * LANES
    step = 64

    def meet(own, group, pieces, total, label, with_sums, fresh=False, between=None):
        mine = held[own, 0, :, 0].reshape(rows, width)
        others = jnp.concatenate([held[group, pair, k].reshape(span, width) for pair, k in pieces], axis=0)
        if len(pieces) <= 2:
            cosines[:, :len(pieces) * span] = lax.dot_general(mine, others, NT, preferred_element_type=jnp.float32)
        for i, (pair, k) in enumerate(pieces):
            here = cosines.at[:, pl.ds((i % 2) * span, span)]
            if len(pieces) > 2 and i % 2 == 0:
                cosines[...] = lax.dot_general(mine, others[i * span:(i + 2) * span], NT, preferred_element_type=jnp.float32)
            for first in range(0, rows, step):
                block = pl.ds(first, step)
                cosine = here[block]
                logits = temp * cosine + shift
                if label is not None:
                    is_pair = label(first, k)
                    logits = jnp.where(is_pair, -logits, logits)
                small = jnp.exp(-jnp.abs(logits))
                upper = 1.0 / (1.0 + small)
                slope = jnp.where(logits >= 0, upper, small * upper)
                if label is not None:
                    slope = jnp.where(is_pair, -slope, slope)
                slopes[block, i * span:(i + 1) * span] = slope.astype(jnp.bfloat16)
                if with_sums:
                    pair_loss = jnp.maximum(logits, 0.0) + jnp.log1p(small)
                    for j, value in enumerate((pair_loss, slope * cosine, slope)):
                        value = jnp.sum(value.reshape(step // 8, 8, span), axis=0)
                        sums[j * 8:(j + 1) * 8] += value[:, :LANES] + value[:, LANES:]
        if between is not None:
            between()
        product = jnp.dot(slopes[:, :len(pieces) * span], others, preferred_element_type=jnp.float32)
        total[...] = product if fresh else total[...] + product

    def text_meets_own(pair, k0, count, fresh=False):
        def label(first, k):
            lane = lax.broadcasted_iota(jnp.int32, (step, LANES), 1) + k * LANES
            at = jnp.concatenate([lane + quarter[pair][core] * rows for core in range(2)], axis=1)
            here = pos_cols[pl.ds(first, step)]
            return jnp.concatenate([here, here], axis=1) == at
        meet(TXT, IMG, [(pair, k0 + i) for i in range(count)], grad_text, label, True, fresh=fresh)

    def image_meets_own(pair, fresh=False):
        def label(first, k):
            at = lax.broadcasted_iota(jnp.int32, (step, span), 0) + (row * rows + first)
            return jnp.broadcast_to(pos_rows[pair, :, pl.ds(k * span, span)], (step, span)) == at
        meet(IMG, TXT, [(pair, k) for k in range(parts)], grad_image, label, False, fresh=fresh)

    image_meets_own(0, True)
    text_meets_own(0, 0, parts, True)
    image_meets_own(1)

    def bytes_of(ref, sent, arrived):
        return pltpu.make_async_remote_copy(src_ref=ref, dst_ref=ref, send_sem=sent, recv_sem=arrived,
                                            device_id=(dp, side), device_id_type=MESH)

    def to_a(i):
        return pltpu.make_async_remote_copy(
            src_ref=packed, dst_ref=met_a.at[place_a], send_sem=send_a, recv_sem=recv_a,
            device_id=group_a[i], device_id_type=MESH)

    def to_b(i):
        return pltpu.make_async_remote_copy(
            src_ref=met_b.at[rest], dst_ref=met_b.at[rest], send_sem=send_b, recv_sem=recv_b,
            device_id=group_b[i], device_id_type=MESH)

    def finish(total, which):
        @pl.loop(0, parts)
        def _(k):
            block = pl.ds(pl.multiple_of(k * LANES, LANES), LANES)
            full = (raw, image)[which][block].astype(jnp.float32)
            grad = temp * total[block]
            inverse = inverses[which, k][:, 0:1]
            unit = full * inverse
            along = jnp.sum(unit * grad, axis=-1, keepdims=True)
            total[block] = (grad - unit * along) * inverse

    own_text.wait()
    packed[...] = jnp.zeros_like(packed)

    @pl.loop(0, parts)
    def _(t):
        def pieces(together):
            return [(jnp.where(together, s % 2, s // parts), jnp.where(together, s // 2, s % parts))
                    for s in (2 * t, 2 * t + 1)]

        nexts, prevs = pieces(last_z), pieces(first_z)
        early = t < parts // 2
        x_two = jnp.logical_and(jnp.logical_not(end_z), early)

        @pl.when(x_two)
        def _():
            for i in range(2):
                x_img(2 * t + i).wait_recv()
                f_img(2 * t + i).start()
                z_img(1, 2 * t + i).start()

        def take_nexts():
            for i in range(2):
                z_img(*nexts[i]).wait_recv()
                f_next(*nexts[i]).start()

                @pl.when(jnp.logical_and(before_last_z, early))
                def _():
                    x_next(nexts[i][1]).start()

        def take_prevs():
            for i in range(2):
                z_txt(*prevs[i]).wait_recv()
                f_prev(*prevs[i]).start()

        def meet_prevs():
            for i in range(2):
                f_prev(*prevs[i]).wait_recv()
            meet(IMG, PREV, prevs, grad_image, None, False)

        last = t == parts - 1

        def start_sums():
            @pl.when(last)
            def _():
                for i in range(3):
                    packed[i:i + 1] = jnp.sum(sums[8 * i:8 * (i + 1)], axis=0, keepdims=True)
                for i in range(len(group_a)):
                    to_a(i).start()

        def meet_nexts(between=None):
            for i in range(2):
                f_next(*nexts[i]).wait_recv()
            meet(TXT, NEXT, nexts, grad_text, None, True, between=between)

        pl.when(jnp.logical_not(last_z))(take_nexts)
        pl.when(jnp.logical_not(first_z))(take_prevs)
        pl.when(last_z)(meet_prevs)
        pl.when(jnp.logical_not(last_z))(meet_nexts)

        @pl.when(x_two)
        def _():
            for i in range(2):
                f_img(2 * t + i).wait_recv()
            text_meets_own(1, 2 * t, 2)

        @pl.when(end_z)
        def _():
            x_img(t).wait_recv()
            f_img(t).start()

        pl.when(first_z)(take_prevs)
        pl.when(last_z)(take_nexts)

        @pl.when(end_z)
        def _():
            f_img(t).wait_recv()
            text_meets_own(1, t, 1)

        pl.when(last_z)(functools.partial(meet_nexts, start_sums))
        pl.when(jnp.logical_not(last_z))(start_sums)

        @pl.when(last)
        def _():
            finish(grad_text, 0)
            met_a[place_a] = packed[...]
            bytes_of(met_a.at[pl.ds(0, len(group_a))], send_a, recv_a).wait_recv()
            met_b[rest] = functools.reduce(lambda a, b: a + b, [met_a[i] for i in range(4 * n_y)])
            for i in range(len(group_b)):
                to_b(i).start()

        pl.when(jnp.logical_not(last_z))(meet_prevs)

    finish(grad_image, 1)
    bytes_of(met_b.at[pl.ds(0, len(group_b))], send_b, recv_b).wait_recv()
    total = functools.reduce(lambda a, b: a + b, [met_b[i] for i in range(n_b)])
    count = rows * 4 * n_dp
    out_sums[...] = total / count
    out_sums[1:2] = temp * total[1:2] / count

    def all_sent(*kinds):
        for kind in kinds:
            bytes_of(raw, send_sem.at[kind], recv_sem.at[0, 0]).wait_send()

    all_sent(C_IMG, F_IMG, F_NEXT, F_NEXT + 1, F_PREV, F_PREV + 1)
    for sends, kinds in ((sends_x, (X_IMG,)), (x_for_side, (FOR_SIDE,)), (before_last_z, (X_NEXT,)),
                         (sends_img, (Z_IMG,)), (jnp.logical_and(sends_img, jnp.logical_not(last_z)), (Z_IMG + 1,)),
                         (img_for_side, (FOR_SIDE + 1, FOR_SIDE + 2)),
                         (sends_txt, (Z_TXT, Z_TXT + 1)), (txt_for_side, (FOR_SIDE + 1, FOR_SIDE + 2))):
        @pl.when(sends)
        def _():
            all_sent(*kinds)

    bytes_of(met_a.at[pl.ds(0, len(group_a))], send_a, recv_a).wait_send()
    bytes_of(met_b.at[pl.ds(0, len(group_b))], send_b, recv_b).wait_send()


def write_out(grad_text, grad_image, sums, out_text, out_image, loss, grad_log_temp, grad_bias, sem):
    part = grad_text.shape[0] // 4
    copies = [pltpu.make_async_copy(source.at[pl.ds(i * part, part)], target.at[pl.ds(i * part, part)], sem.at[4 * j + i])
              for j, (source, target) in enumerate(((grad_text, out_text), (grad_image, out_image))) for i in range(4)]
    for copy in copies:
        copy.start()
    for j, out in enumerate((loss, grad_log_temp, grad_bias)):
        out[0] = jnp.sum(sums[j:j + 1])
    for copy in copies:
        copy.wait()


def on_device(n_dp, text, image, positive, log_temp, bias):
    rows, width = image.shape
    parts = rows // LANES
    n_b = min(n_dp, 8)
    n_a = 4 * (n_dp // n_b)
    vmem, smem, hbm = (pl.BlockSpec(memory_space=m) for m in (pltpu.VMEM, pltpu.SMEM, pltpu.HBM))
    dma = pltpu.SemaphoreType.DMA
    results = pl.pallas_call(
        functools.partial(kernel, n_dp),
        out_shape=(
            jax.ShapeDtypeStruct((rows, width), jnp.float32),
            jax.ShapeDtypeStruct((rows, width), jnp.float32),
            jax.ShapeDtypeStruct((8, LANES), jnp.float32),
        ),
        in_specs=[hbm, vmem, hbm, smem, smem],
        out_specs=(vmem, vmem, vmem),
        scratch_shapes=[
            pltpu.VMEM((4, 2, parts, 2, LANES, width), jnp.bfloat16),
            pltpu.VMEM((rows, width), jnp.bfloat16),
            pltpu.VMEM((2, parts, LANES, LANES), jnp.float32),
            pltpu.VMEM((rows, 4 * LANES), jnp.float32),
            pltpu.VMEM((rows, 2 * rows), jnp.bfloat16),
            pltpu.VMEM((1, 4 * rows), jnp.int32),
            pltpu.VMEM((rows, LANES), jnp.int32),
            pltpu.VMEM((2, 1, 2 * rows), jnp.int32),
            pltpu.VMEM((24, LANES), jnp.float32),
            pltpu.VMEM((8, LANES), jnp.float32),
            pltpu.VMEM((n_a, 8, LANES), jnp.float32),
            pltpu.VMEM((n_b, 8, LANES), jnp.float32),
            dma((4, parts)), dma((2,)), dma((KINDS + 4,)), dma((KINDS, parts)),
            *(dma(()),) * 4,
        ],
        compiler_params=pltpu.CompilerParams(
            collective_id=0, has_side_effects=True, vmem_limit_bytes=48 * 1024 * 1024),
        cost_estimate=pl.CostEstimate(
            flops=2 * 32 * rows * rows * width, bytes_accessed=7 * rows * width * 2 + 2 * rows * width * 4,
            transcendentals=24 * rows * rows),
    )(text, image, positive, log_temp, bias)
    scalar = jax.ShapeDtypeStruct((1,), jnp.float32)
    return pl.pallas_call(
        write_out,
        out_shape=(*(jax.ShapeDtypeStruct((rows, width), jnp.float32),) * 2, scalar, scalar, scalar),
        in_specs=[vmem, vmem, vmem],
        out_specs=(hbm, hbm, smem, smem, smem),
        scratch_shapes=[dma((8,))],
        compiler_params=pltpu.CompilerParams(vmem_limit_bytes=1024 * 1024),
    )(*results)


def solution(mesh):
    return jax.shard_map(
        functools.partial(on_device, mesh.shape["dp"]),
        mesh=mesh,
        in_specs=(P("dp", None), P(("dp", "row"), None), P("dp", None), P(), P()),
        out_specs=(P(("dp", "row"), None), P(("dp", "row"), None), P(), P(), P()),
        check_vma=False,
    )
```
